32 devices in a mesh: chan: 16 (over z, x, core), tm: 2 (over y).
Axes of the slice: x: 2, y: 2, z: 4, core: 2. Of those that a mesh axis runs over, the one named last changes fastest.
Arguments:
- voltages: int32 [2, 64, 262144], P(None, 'chan', 'tm'), may hold values from -8 to 7
Outputs:
- visibilities: float32 [2, 1024, 64, 64], P(None, 'chan', 'tm')
The draws below stay inside these ranges and needn't reach their ends.
Inputs may be any that keep to these rules, and one draw needn't show every extreme that they name: `voltages`: 4-bit two's complement samples.
All inputs are finite; a program needn't handle non-finite values.
Results may differ from the reference program's by a relative error of at most 0.001.
Values may be sent and summed in bfloat16 or wider, within the bound.
A program may use at most 128 MiB of HBM per device.

```python
import jax
import jax.numpy as jnp
from jax import lax

NCH = 1024
TAPS = 4
INPUTS = 64
NTOT = 256
SAMPLES = 262144


def place_ends(values, own_key, low, largest):
    longest = values.shape.index(max(values.shape))
    spots = []
    for shift in (0, 1):
        where = [jax.random.randint(jax.random.fold_in(own_key, axis), (), 0, length) for axis, length in enumerate(values.shape)]
        where[longest] = (where[longest] + shift) % values.shape[longest]
        spots.append(tuple(where))
    return values.at[spots[0]].set(low).at[spots[1]].set(largest)


def setup_inputs(seed: int = 0) -> dict:
    keys = jax.random.split(jax.random.key(seed), 2)
    voltages = place_ends(jax.random.randint(keys[0], (2, INPUTS, SAMPLES), -8, 8), jax.random.fold_in(keys[0], 1), -8, 7).astype(jnp.int32)
    return {"voltages": voltages}


def make_taps(nch):
    k = jnp.arange(TAPS * nch, dtype=jnp.float32)
    x = (k - 2.0 * nch + 0.5) / nch
    window = 0.54 - 0.46 * jnp.cos(2.0 * jnp.pi * (k + 0.5) / (TAPS * nch))
    return (jnp.sinc(x) * window).reshape(TAPS, nch)

def correlate_block(block):
    real_part = block[:, 0].astype(jnp.float32)
    imag_part = block[:, 1].astype(jnp.float32)
    vis_real = jnp.einsum('cas,cbs->cab', real_part, real_part) + jnp.einsum('cas,cbs->cab', imag_part, imag_part)
    vis_imag = jnp.einsum('cas,cbs->cab', imag_part, real_part) - jnp.einsum('cas,cbs->cab', real_part, imag_part)
    return jnp.stack([vis_real, vis_imag], axis=0)

def reference(voltages):
    samples = voltages.astype(jnp.float32) * 0.25
    frames = samples.reshape(2, INPUTS, NTOT, NCH)
    padded = jnp.concatenate([jnp.zeros((2, INPUTS, TAPS - 1, NCH), jnp.float32), frames], axis=2)
    taps = make_taps(NCH)
    filtered = taps[0] * padded[:, :, 0:NTOT, :]
    for step in range(1, TAPS):
        filtered = filtered + taps[step] * padded[:, :, step:step + NTOT, :]
    spectra = jnp.fft.fft(filtered[0] + 1j * filtered[1], axis=-1) / jnp.sqrt(jnp.float32(NCH))
    spec_real = jnp.real(spectra).astype(jnp.bfloat16)
    spec_imag = jnp.imag(spectra).astype(jnp.bfloat16)
    stacked = jnp.stack([spec_real, spec_imag], axis=0)
    by_channel = jnp.transpose(stacked, (3, 0, 1, 2)).reshape(NCH // 8, 8, 2, INPUTS, NTOT)
    result = lax.map(correlate_block, by_channel)
    result = jnp.transpose(result, (1, 0, 2, 3, 4)).reshape(2, NCH, INPUTS, INPUTS)
    return result * (1.0 / NTOT)
```

```python
import functools

import jax
import jax.numpy as jnp
import ml_dtypes
import numpy as np
from jax import lax
from jax.experimental import pallas as pl
from jax.experimental.pallas import tpu as pltpu
from jax.sharding import PartitionSpec as P

NCH = 1024
TAPS = 4
RADIX = 4
GROUP = 16
NT = (((1,), (1,)), ((), ()))


def make_taps(nch):
    k = np.arange(TAPS * nch, dtype=np.float64)
    x = (k - 2.0 * nch + 0.5) / nch
    window = 0.54 - 0.46 * np.cos(2.0 * np.pi * (k + 0.5) / (TAPS * nch))
    return (np.sinc(x) * window).reshape(TAPS, nch).astype(np.float32)


def make_dft(nch):
    sub = nch // RADIX
    n = np.arange(sub)
    highs, lows = [], []
    for r in range(RADIX):
        k = RADIX * np.arange(sub) + r
        angle = (k[:, None] * n[None, :] % nch) * (2.0 * np.pi / nch)
        c, s = np.cos(angle), np.sin(angle)
        m = np.block([[c, s], [-s, c]]) * (0.25 / np.sqrt(nch))
        high = m.astype(np.float32).astype(ml_dtypes.bfloat16)
        low = (m - high.astype(np.float64)).astype(np.float32).astype(ml_dtypes.bfloat16)
        highs.append(high)
        lows.append(low)
    return np.stack(highs), np.stack(lows)


def make_permutation(local_inputs):
    size = GROUP * 4 * local_inputs
    order = np.arange(size).reshape(GROUP, 2, 2, local_inputs).transpose(1, 2, 0, 3).reshape(-1)
    perm = np.zeros((size, size), np.float32)
    perm[np.arange(size), order] = 1.0
    return perm.astype(ml_dtypes.bfloat16)


def kernel(
    n,
    raw_ref,
    halo_ref,
    taps_ref,
    high_ref,
    low_ref,
    perm_ref,
    out_ref,
    ext,
    y_high,
    y_low,
    spread,
    send,
    recv,
    part,
    other,
    send_sem,
    recv_sem,
    tm_send_sem,
    tm_recv_sem,
):
    me = lax.axis_index("chan")
    t = lax.axis_index("tm")
    inputs, specs = raw_ref.shape[1], raw_ref.shape[2]
    sub = NCH // RADIX
    rows = send.shape[2]
    pairs = rows // (4 * inputs)
    groups = n // GROUP
    total = n * inputs
    half = total // 2

    barrier = pltpu.get_barrier_semaphore()

    @pl.loop(1, n)
    def _(i):
        pl.semaphore_signal(barrier, inc=1, device_id={"chan": lax.rem(me + i, n)}, device_id_type=pl.DeviceIdType.MESH)

    pl.semaphore_signal(barrier, inc=1, device_id={"tm": 1 - t}, device_id_type=pl.DeviceIdType.MESH)

    @pl.loop(0, inputs)
    def _(a):
        at = pl.multiple_of(a * specs, specs)
        for p in range(2):
            ext[p, 0:8, :] = halo_ref[p, a].astype(jnp.float32)
            ext[p, 8 : 8 + specs, :] = raw_ref[p, a].astype(jnp.float32)
        quarters = []
        for p in range(2):
            row = []
            for q in range(RADIX):
                lanes = slice(q * sub, (q + 1) * sub)
                value = taps_ref[0:1, lanes] * ext[p, 5 : 5 + specs, lanes]
                for step in range(1, TAPS):
                    value = value + taps_ref[step : step + 1, lanes] * ext[p, 5 + step : 5 + step + specs, lanes]
                row.append(value)
            quarters.append(row)
        r, im = quarters
        er, orr, dr, gr = r[0] + r[2], r[1] + r[3], r[0] - r[2], r[1] - r[3]
        ei, oi, di, gi = im[0] + im[2], im[1] + im[3], im[0] - im[2], im[1] - im[3]
        parts = [(er + orr, ei + oi), (dr + gi, di - gr), (er - orr, ei - oi), (dr - gi, di + gr)]
        for k1 in range(RADIX):
            for p in range(2):
                value = parts[k1][p]
                high = value.astype(jnp.bfloat16)
                low = (value - high.astype(jnp.float32)).astype(jnp.bfloat16)
                y_high[k1, pl.ds(at, specs), p * sub : (p + 1) * sub] = high
                y_low[k1, pl.ds(at, specs), p * sub : (p + 1) * sub] = low

    pl.semaphore_wait(barrier, n)

    @pl.loop(0, RADIX)
    def _(k1):
        for p in range(2):
            mine = slice(p * sub, (p + 1) * sub)
            mh, ml = high_ref[k1, mine, :], low_ref[k1, mine, :]
            yh, yl = y_high[k1], y_low[k1]
            value = lax.dot_general(mh, yh, NT, preferred_element_type=jnp.float32)
            value = value + lax.dot_general(mh, yl, NT, preferred_element_type=jnp.float32)
            value = value + lax.dot_general(ml, yh, NT, preferred_element_type=jnp.float32)
            for a in range(inputs):
                spread[pl.ds(p * inputs + a, sub, 2 * inputs), :] = value[:, a * specs : (a + 1) * specs]
        send[k1] = spread[...].astype(jnp.bfloat16).reshape(n, rows, specs)
        pltpu.make_async_copy(send.at[k1, me], recv.at[k1, me], recv_sem.at[k1]).start()

        @pl.loop(1, n)
        def _(i):
            to = lax.rem(me + i, n)
            pltpu.make_async_remote_copy(
                src_ref=send.at[k1, to],
                dst_ref=recv.at[k1, me],
                send_sem=send_sem.at[k1],
                recv_sem=recv_sem.at[k1],
                device_id={"chan": to},
                device_id_type=pl.DeviceIdType.MESH,
            ).start()

    def exchange(k1):
        return pltpu.make_async_remote_copy(
            src_ref=part.at[k1, :, pl.ds(pl.multiple_of((1 - t) * half, half), half), :],
            dst_ref=other.at[k1],
            send_sem=tm_send_sem.at[k1],
            recv_sem=tm_recv_sem.at[k1],
            device_id={"tm": 1 - t},
            device_id_type=pl.DeviceIdType.MESH,
        )

    def finish(k1):
        exchange(k1).wait_recv()
        own = part[k1, :, pl.ds(pl.multiple_of(t * half, half), half), :]
        out_ref[:, k1] = (own + other[k1]) * (1.0 / (2 * specs))

    @pl.loop(0, RADIX)
    def _(k1):
        pltpu.make_async_copy(recv.at[k1], recv.at[k1], recv_sem.at[k1]).wait()

        @pl.loop(0, pairs)
        def _(j):
            at = pl.multiple_of(j * 4 * inputs, 4 * inputs)
            turned = []
            for g in range(groups):
                block = recv[k1, g * GROUP : (g + 1) * GROUP, pl.ds(at, 4 * inputs), :].reshape(GROUP * 4 * inputs, specs)
                turned.append(jnp.dot(perm_ref[...], block, preferred_element_type=jnp.float32).astype(jnp.bfloat16))
            run = GROUP * inputs
            for c in range(2):
                real = jnp.concatenate([x[2 * c * run : (2 * c + 1) * run] for x in turned], axis=0)
                imag = jnp.concatenate([x[(2 * c + 1) * run : (2 * c + 2) * run] for x in turned], axis=0)
                left = jnp.concatenate([real, imag], axis=1)
                right = jnp.concatenate([left, jnp.concatenate([-imag, real], axis=1)], axis=0)
                part[k1, 2 * j + c] = lax.dot_general(left, right, NT, preferred_element_type=jnp.float32)

        exchange(k1).start()

        @pl.when(k1 > 0)
        def _():
            finish(k1 - 1)

    finish(RADIX - 1)

    @pl.loop(0, RADIX)
    def _(k1):
        exchange(k1).wait_send()
        pltpu.make_async_copy(send.at[k1, 0 : n - 1], send.at[k1, 0 : n - 1], send_sem.at[k1]).wait()


def local(n, voltages):
    inputs = voltages.shape[1]
    specs = voltages.shape[2] // NCH
    raw = voltages.reshape(2, inputs, specs, NCH)
    halo = lax.ppermute(raw[:, :, specs - 8 :, :], "tm", [(0, 1)])
    high, low = make_dft(NCH)
    chans = NCH // n
    per = chans // RADIX
    total = n * inputs
    rows = per * 2 * inputs
    whole = pl.BlockSpec(memory_space=pltpu.VMEM)
    out = pl.pallas_call(
        functools.partial(kernel, n),
        out_shape=jax.ShapeDtypeStruct((per, RADIX, total // 2, 2 * total), jnp.float32),
        in_specs=[whole] * 6,
        out_specs=whole,
        scratch_shapes=[
            pltpu.VMEM((2, specs + 8, NCH), jnp.float32),
            pltpu.VMEM((RADIX, inputs * specs, NCH // 2), jnp.bfloat16),
            pltpu.VMEM((RADIX, inputs * specs, NCH // 2), jnp.bfloat16),
            pltpu.VMEM((NCH // RADIX * 2 * inputs, specs), jnp.float32),
            pltpu.VMEM((RADIX, n, rows, specs), jnp.bfloat16),
            pltpu.VMEM((RADIX, n, rows, specs), jnp.bfloat16),
            pltpu.VMEM((RADIX, per, total, 2 * total), jnp.float32),
            pltpu.VMEM((RADIX, per, total // 2, 2 * total), jnp.float32),
            pltpu.SemaphoreType.DMA((RADIX,)),
            pltpu.SemaphoreType.DMA((RADIX,)),
            pltpu.SemaphoreType.DMA((RADIX,)),
            pltpu.SemaphoreType.DMA((RADIX,)),
        ],
        compiler_params=pltpu.CompilerParams(
            collective_id=0, has_side_effects=True, vmem_limit_bytes=60 * 1024 * 1024
        ),
    )(raw, halo, jnp.asarray(make_taps(NCH)), jnp.asarray(high), jnp.asarray(low), jnp.asarray(make_permutation(inputs)))
    out = out.reshape(chans, total // 2, 2, total)
    return jnp.transpose(out, (2, 0, 1, 3))


def solution(mesh):
    placed = (P(None, "chan", "tm"),)
    return jax.shard_map(
        functools.partial(local, mesh.shape["chan"]),
        mesh=mesh,
        in_specs=placed,
        out_specs=P(None, "chan", "tm", None),
        check_vma=False,
    )
```

```python
import functools

import jax
import jax.numpy as jnp
import ml_dtypes
import numpy as np
from jax import lax
from jax.experimental import pallas as pl
from jax.experimental.pallas import tpu as pltpu
from jax.sharding import PartitionSpec as P

NCH = 1024
TAPS = 4
RADIX = 4
GROUP = 16
LANES = 128
BLOCK = 16
SPLIT = 2
NT = (((1,), (1,)), ((), ()))


def make_taps(nch):
    k = np.arange(TAPS * nch, dtype=np.float64)
    x = (k - 2.0 * nch + 0.5) / nch
    window = 0.54 - 0.46 * np.cos(2.0 * np.pi * (k + 0.5) / (TAPS * nch))
    return (np.sinc(x) * window).reshape(TAPS, nch).astype(np.float32)


def make_dft(nch):
    sub = nch // RADIX
    n = np.arange(sub)
    highs, lows = [], []
    for r in range(RADIX):
        k = RADIX * np.arange(sub) + r
        angle = (k[:, None] * n[None, :] % nch) * (2.0 * np.pi / nch)
        c, s = np.cos(angle), np.sin(angle)
        m = np.block([[c, s], [-s, c]]) * (0.25 / np.sqrt(nch))
        high = m.astype(np.float32).astype(ml_dtypes.bfloat16)
        low = (m - high.astype(np.float64)).astype(np.float32).astype(ml_dtypes.bfloat16)
        highs.append(high)
        lows.append(low)
    return np.stack(highs), np.stack(lows)


def make_permutation(local_inputs):
    size = GROUP * 4 * local_inputs
    order = np.arange(size).reshape(GROUP, 2, 2, local_inputs).transpose(1, 2, 0, 3).reshape(-1)
    perm = np.zeros((size, size), np.float32)
    perm[np.arange(size), order] = 1.0
    return perm.astype(ml_dtypes.bfloat16)


def kernel(
    n,
    inputs,
    specs,
    volts_ref,
    taps_ref,
    high_ref,
    low_ref,
    perm_ref,
    out_ref,
    raw,
    high,
    low,
    filtered,
    y_high,
    y_low,
    spread,
    send,
    recv,
    part,
    other,
    load_sem,
    table_sem,
    halo_send_sem,
    halo_recv_sem,
    send_sem,
    recv_sem,
    tm_send_sem,
    tm_recv_sem,
):
    me = lax.axis_index("chan")
    t = lax.axis_index("tm")
    sub = NCH // RADIX
    tiles = NCH // LANES
    frame = tiles * inputs
    before = (TAPS - 1) * frame
    chunks = recv.shape[0]
    split = chunks // RADIX
    rows = recv.shape[2]
    pairs = rows // (4 * inputs)
    groups = n // GROUP
    half = n * inputs // 2

    barrier = pltpu.get_barrier_semaphore()

    @pl.loop(1, n)
    def _(i):
        pl.semaphore_signal(barrier, inc=1, device_id={"chan": lax.rem(me + i, n)}, device_id_type=pl.DeviceIdType.MESH)

    pl.semaphore_signal(barrier, inc=1, device_id={"tm": 1 - t}, device_id_type=pl.DeviceIdType.MESH)

    loads = [
        pltpu.make_async_copy(volts_ref.at[p], raw.at[p, before : before + specs * frame, :], load_sem.at[p])
        for p in range(2)
    ]
    tables = [
        pltpu.make_async_copy(high_ref, high, table_sem.at[0]),
        pltpu.make_async_copy(low_ref, low, table_sem.at[1]),
    ]
    for copy in loads + tables:
        copy.start()

    halo = pltpu.make_async_remote_copy(
        src_ref=volts_ref.at[:, specs * frame - before : specs * frame, :],
        dst_ref=raw.at[:, 0:before, :],
        send_sem=halo_send_sem,
        recv_sem=halo_recv_sem,
        device_id={"tm": 1 - t},
        device_id_type=pl.DeviceIdType.MESH,
    )
    pl.semaphore_wait(barrier, n)

    @pl.when(t == 0)
    def _():
        halo.start()
        raw[:, 0:before, :] = jnp.zeros((2, before, LANES), jnp.int32)

    for copy in loads:
        copy.wait()

    def filter_block(b, a):
        at = b * BLOCK
        for p in range(2):
            frames = raw[p, pl.ds(at * frame + a, (BLOCK + TAPS - 1) * tiles, inputs), :].astype(jnp.float32)
            frames = frames.reshape(BLOCK + TAPS - 1, tiles, LANES)
            value = taps_ref[0] * frames[0:BLOCK]
            for step in range(1, TAPS):
                value = value + taps_ref[step] * frames[step : step + BLOCK]
            filtered[p] = value.reshape(BLOCK * tiles, LANES)
        quarter = tiles // RADIX
        place = pl.ds(pl.multiple_of(a * specs + at, BLOCK), BLOCK)
        for h in range(quarter):
            r, im = [[filtered[p, pl.ds(q * quarter + h, BLOCK, tiles), :] for q in range(RADIX)] for p in range(2)]
            er, orr, dr, gr = r[0] + r[2], r[1] + r[3], r[0] - r[2], r[1] - r[3]
            ei, oi, di, gi = im[0] + im[2], im[1] + im[3], im[0] - im[2], im[1] - im[3]
            parts = [(er + orr, ei + oi), (dr + gi, di - gr), (er - orr, ei - oi), (dr - gi, di + gr)]
            for k1 in range(RADIX):
                for p in range(2):
                    value = parts[k1][p]
                    top = value.astype(jnp.bfloat16)
                    lanes = slice(p * sub + h * LANES, p * sub + (h + 1) * LANES)
                    y_high[k1, place, lanes] = top
                    y_low[k1, place, lanes] = (value - top.astype(jnp.float32)).astype(jnp.bfloat16)

    @pl.loop(1, specs // BLOCK)
    def _(b):
        for a in range(inputs):
            filter_block(b, a)

    @pl.when(t == 1)
    def _():
        halo.wait_recv()

    for a in range(inputs):
        filter_block(0, a)

    for copy in tables:
        copy.wait()

    @pl.loop(0, RADIX)
    def _(k1):
        for p in range(2):
            mine = slice(p * sub, (p + 1) * sub)
            mh, ml = high[k1, mine, :], low[k1, mine, :]
            yh, yl = y_high[k1], y_low[k1]
            value = lax.dot_general(mh, yh, NT, preferred_element_type=jnp.float32)
            value = value + lax.dot_general(mh, yl, NT, preferred_element_type=jnp.float32)
            value = value + lax.dot_general(ml, yh, NT, preferred_element_type=jnp.float32)
            for a in range(inputs):
                spread[pl.ds(p * inputs + a, sub, 2 * inputs), :] = value[:, a * specs : (a + 1) * specs]
        send[k1] = spread[...].astype(jnp.bfloat16).reshape(n, split * rows, specs)
        for h in range(split):
            chunk = k1 * split + h
            cut = pl.ds(h * rows, rows)
            pltpu.make_async_copy(send.at[k1, me, cut], recv.at[chunk, me], recv_sem.at[chunk]).start()

            @pl.loop(0, n - 1)
            def _(i):
                step = (i + 1) // 2
                to = lax.rem(me + n + n // 2 + step * (2 * (i % 2) - 1), n)
                pltpu.make_async_remote_copy(
                    src_ref=send.at[k1, to, cut],
                    dst_ref=recv.at[chunk, me],
                    send_sem=send_sem.at[k1],
                    recv_sem=recv_sem.at[chunk],
                    device_id={"chan": to},
                    device_id_type=pl.DeviceIdType.MESH,
                ).start()

    def exchange(chunk):
        return pltpu.make_async_remote_copy(
            src_ref=part.at[chunk, :, pl.ds(pl.multiple_of((1 - t) * half, half), half), :],
            dst_ref=other.at[chunk],
            send_sem=tm_send_sem.at[chunk],
            recv_sem=tm_recv_sem.at[chunk],
            device_id={"tm": 1 - t},
            device_id_type=pl.DeviceIdType.MESH,
        )

    def finish(chunk):
        exchange(chunk).wait_recv()
        own = part[chunk, :, pl.ds(pl.multiple_of(t * half, half), half), :]
        out_ref[chunk % split, :, chunk // split] = (own + other[chunk]) * (1.0 / (2 * specs))

    @pl.loop(0, chunks)
    def _(chunk):
        pltpu.make_async_copy(recv.at[chunk], recv.at[chunk], recv_sem.at[chunk]).wait()

        @pl.loop(0, pairs)
        def _(j):
            at = pl.multiple_of(j * 4 * inputs, 4 * inputs)
            turned = []
            for g in range(groups):
                block = recv[chunk, g * GROUP : (g + 1) * GROUP, pl.ds(at, 4 * inputs), :]
                block = block.reshape(GROUP * 4 * inputs, specs)
                turned.append(jnp.dot(perm_ref[...], block, preferred_element_type=jnp.float32).astype(jnp.bfloat16))
            run = GROUP * inputs
            for c in range(2):
                real = jnp.concatenate([x[2 * c * run : (2 * c + 1) * run] for x in turned], axis=0)
                imag = jnp.concatenate([x[(2 * c + 1) * run : (2 * c + 2) * run] for x in turned], axis=0)
                left = jnp.concatenate([real, imag], axis=1)
                right = jnp.concatenate([left, jnp.concatenate([-imag, real], axis=1)], axis=0)
                part[chunk, 2 * j + c] = lax.dot_general(left, right, NT, preferred_element_type=jnp.float32)

        exchange(chunk).start()

        @pl.when(chunk > 0)
        def _():
            finish(chunk - 1)

    finish(chunks - 1)

    @pl.when(t == 0)
    def _():
        halo.wait_send()

    @pl.loop(0, chunks)
    def _(chunk):
        exchange(chunk).wait_send()

    @pl.loop(0, RADIX)
    def _(k1):
        pltpu.make_async_copy(send.at[k1, 0 : n - 1], send.at[k1, 0 : n - 1], send_sem.at[k1]).wait()


def local(n, voltages):
    inputs = voltages.shape[1]
    specs = voltages.shape[2] // NCH
    tiles = NCH // LANES
    frame = tiles * inputs
    volts = voltages.reshape(2, inputs, specs * tiles, LANES).transpose(0, 2, 1, 3).reshape(2, specs * frame, LANES)
    high, low = make_dft(NCH)
    per = NCH // n // RADIX
    split = SPLIT if per % (2 * SPLIT) == 0 else 1
    chunks, each = RADIX * split, per // split
    total = n * inputs
    rows = each * 2 * inputs
    whole = pl.BlockSpec(memory_space=pltpu.VMEM)
    there = pl.BlockSpec(memory_space=pl.ANY)
    out = pl.pallas_call(
        functools.partial(kernel, n, inputs, specs),
        out_shape=jax.ShapeDtypeStruct((split, each, RADIX, total // 2, 2 * total), jnp.float32),
        in_specs=[there, whole, there, there, whole],
        out_specs=whole,
        scratch_shapes=[
            pltpu.VMEM((2, (specs + TAPS - 1) * frame, LANES), jnp.int32),
            pltpu.VMEM((RADIX, NCH // 2, NCH // 2), jnp.bfloat16),
            pltpu.VMEM((RADIX, NCH // 2, NCH // 2), jnp.bfloat16),
            pltpu.VMEM((2, BLOCK * tiles, LANES), jnp.float32),
            pltpu.VMEM((RADIX, inputs * specs, NCH // 2), jnp.bfloat16),
            pltpu.VMEM((RADIX, inputs * specs, NCH // 2), jnp.bfloat16),
            pltpu.VMEM((NCH // RADIX * 2 * inputs, specs), jnp.float32),
            pltpu.VMEM((RADIX, n, split * rows, specs), jnp.bfloat16),
            pltpu.VMEM((chunks, n, rows, specs), jnp.bfloat16),
            pltpu.VMEM((chunks, each, total, 2 * total), jnp.float32),
            pltpu.VMEM((chunks, each, total // 2, 2 * total), jnp.float32),
            pltpu.SemaphoreType.DMA((2,)),
            pltpu.SemaphoreType.DMA((2,)),
            pltpu.SemaphoreType.DMA,
            pltpu.SemaphoreType.DMA,
            pltpu.SemaphoreType.DMA((RADIX,)),
            pltpu.SemaphoreType.DMA((chunks,)),
            pltpu.SemaphoreType.DMA((chunks,)),
            pltpu.SemaphoreType.DMA((chunks,)),
        ],
        compiler_params=pltpu.CompilerParams(
            collective_id=0, has_side_effects=True, vmem_limit_bytes=60 * 1024 * 1024
        ),
    )(
        volts,
        jnp.asarray(make_taps(NCH).reshape(TAPS, tiles, LANES)),
        jnp.asarray(high),
        jnp.asarray(low),
        jnp.asarray(make_permutation(inputs)),
    )
    out = out.reshape(1, RADIX * per, total // 2, 2 * total)
    first = lax.broadcasted_iota(jnp.int32, (2, 1, 1, 1), 0) == 0
    return jnp.where(first, out[..., :total], out[..., total:])


def solution(mesh):
    placed = (P(None, "chan", "tm"),)
    return jax.shard_map(
        functools.partial(local, mesh.shape["chan"]),
        mesh=mesh,
        in_specs=placed,
        out_specs=P(None, "chan", "tm", None),
        check_vma=False,
    )
```

```python
import functools

import jax
import jax.numpy as jnp
import ml_dtypes
import numpy as np
from jax import lax
from jax.experimental import pallas as pl
from jax.experimental.pallas import tpu as pltpu
from jax.sharding import PartitionSpec as P

NCH = 1024
TAPS = 4
RADIX = 4
GROUP = 16
LANES = 128
BLOCK = 16
SPLIT = 2
NT = (((1,), (1,)), ((), ()))


def make_taps(nch):
    k = np.arange(TAPS * nch, dtype=np.float64)
    x = (k - 2.0 * nch + 0.5) / nch
    window = 0.54 - 0.46 * np.cos(2.0 * np.pi * (k + 0.5) / (TAPS * nch))
    return (np.sinc(x) * window).reshape(TAPS, nch).astype(np.float32)


def make_dft(nch):
    sub = nch // RADIX
    n = np.arange(sub)
    highs, lows = [], []
    for r in range(RADIX):
        k = RADIX * np.arange(sub) + r
        angle = (k[:, None] * n[None, :] % nch) * (2.0 * np.pi / nch)
        c, s = np.cos(angle), np.sin(angle)
        m = np.block([[c, s], [-s, c]]) * (0.25 / np.sqrt(nch))
        high = m.astype(np.float32).astype(ml_dtypes.bfloat16)
        low = (m - high.astype(np.float64)).astype(np.float32).astype(ml_dtypes.bfloat16)
        highs.append(high)
        lows.append(low)
    return np.stack(highs), np.stack(lows)


def make_permutation(local_inputs):
    size = GROUP * 4 * local_inputs
    order = np.arange(size).reshape(GROUP, 2, 2, local_inputs).transpose(1, 2, 0, 3).reshape(-1)
    perm = np.zeros((size, size), np.float32)
    perm[np.arange(size), order] = 1.0
    return perm.astype(ml_dtypes.bfloat16)


def filter_block(b, a, inputs, specs, raw, taps_ref, filtered, y_high, y_low):
    sub = NCH // RADIX
    tiles = NCH // LANES
    frame = tiles * inputs
    at = b * BLOCK
    for p in range(2):
        frames = raw[p, pl.ds(at * frame + a, (BLOCK + TAPS - 1) * tiles, inputs), :].astype(jnp.float32)
        frames = frames.reshape(BLOCK + TAPS - 1, tiles, LANES)
        value = taps_ref[0] * frames[0:BLOCK]
        for step in range(1, TAPS):
            value = value + taps_ref[step] * frames[step : step + BLOCK]
        filtered[p] = value.reshape(BLOCK * tiles, LANES)
    quarter = tiles // RADIX
    place = pl.ds(pl.multiple_of(a * specs + at, BLOCK), BLOCK)
    for h in range(quarter):
        r, im = [[filtered[p, pl.ds(q * quarter + h, BLOCK, tiles), :] for q in range(RADIX)] for p in range(2)]
        er, orr, dr, gr = r[0] + r[2], r[1] + r[3], r[0] - r[2], r[1] - r[3]
        ei, oi, di, gi = im[0] + im[2], im[1] + im[3], im[0] - im[2], im[1] - im[3]
        parts = [(er + orr, ei + oi), (dr + gi, di - gr), (er - orr, ei - oi), (dr - gi, di + gr)]
        for k1 in range(RADIX):
            for p in range(2):
                value = parts[k1][p]
                top = value.astype(jnp.bfloat16)
                lanes = slice(p * sub + h * LANES, p * sub + (h + 1) * LANES)
                y_high[k1, place, lanes] = top
                y_low[k1, place, lanes] = (value - top.astype(jnp.float32)).astype(jnp.bfloat16)


def kernel_few(
    n,
    inputs,
    specs,
    volts_ref,
    taps_ref,
    high_ref,
    low_ref,
    perm_ref,
    out_ref,
    raw,
    high,
    low,
    filtered,
    y_high,
    y_low,
    spread,
    send,
    recv,
    part,
    other,
    load_sem,
    table_sem,
    halo_send_sem,
    halo_recv_sem,
    send_sem,
    recv_sem,
    tm_send_sem,
    tm_recv_sem,
):
    me = lax.axis_index("chan")
    t = lax.axis_index("tm")
    sub = NCH // RADIX
    tiles = NCH // LANES
    frame = tiles * inputs
    before = (TAPS - 1) * frame
    chunks = recv.shape[0]
    split = chunks // RADIX
    rows = recv.shape[2]
    pairs = rows // (4 * inputs)
    groups = n // GROUP
    half = n * inputs // 2

    barrier = pltpu.get_barrier_semaphore()

    @pl.loop(1, n)
    def _(i):
        pl.semaphore_signal(barrier, inc=1, device_id={"chan": lax.rem(me + i, n)}, device_id_type=pl.DeviceIdType.MESH)

    pl.semaphore_signal(barrier, inc=1, device_id={"tm": 1 - t}, device_id_type=pl.DeviceIdType.MESH)

    loads = [
        pltpu.make_async_copy(volts_ref.at[p], raw.at[p, before : before + specs * frame, :], load_sem.at[p])
        for p in range(2)
    ]
    tables = [
        pltpu.make_async_copy(high_ref, high, table_sem.at[0]),
        pltpu.make_async_copy(low_ref, low, table_sem.at[1]),
    ]
    for copy in loads + tables:
        copy.start()

    halo = pltpu.make_async_remote_copy(
        src_ref=volts_ref.at[:, specs * frame - before : specs * frame, :],
        dst_ref=raw.at[:, 0:before, :],
        send_sem=halo_send_sem,
        recv_sem=halo_recv_sem,
        device_id={"tm": 1 - t},
        device_id_type=pl.DeviceIdType.MESH,
    )
    pl.semaphore_wait(barrier, n)

    @pl.when(t == 0)
    def _():
        halo.start()
        raw[:, 0:before, :] = jnp.zeros((2, before, LANES), jnp.int32)

    for copy in loads:
        copy.wait()

    @pl.loop(1, specs // BLOCK)
    def _(b):
        for a in range(inputs):
            filter_block(b, a, inputs, specs, raw, taps_ref, filtered, y_high, y_low)

    @pl.when(t == 1)
    def _():
        halo.wait_recv()

    for a in range(inputs):
        filter_block(0, a, inputs, specs, raw, taps_ref, filtered, y_high, y_low)

    for copy in tables:
        copy.wait()

    @pl.loop(0, RADIX)
    def _(k1):
        for p in range(2):
            mine = slice(p * sub, (p + 1) * sub)
            mh, ml = high[k1, mine, :], low[k1, mine, :]
            yh, yl = y_high[k1], y_low[k1]
            value = lax.dot_general(mh, yh, NT, preferred_element_type=jnp.float32)
            value = value + lax.dot_general(mh, yl, NT, preferred_element_type=jnp.float32)
            value = value + lax.dot_general(ml, yh, NT, preferred_element_type=jnp.float32)
            for a in range(inputs):
                spread[pl.ds(p * inputs + a, sub, 2 * inputs), :] = value[:, a * specs : (a + 1) * specs]
        send[k1] = spread[...].astype(jnp.bfloat16).reshape(n, split * rows, specs)
        for h in range(split):
            chunk = k1 * split + h
            cut = pl.ds(h * rows, rows)
            pltpu.make_async_copy(send.at[k1, me, cut], recv.at[chunk, me], recv_sem.at[chunk]).start()

            @pl.loop(0, n - 1)
            def _(i):
                step = (i + 1) // 2
                to = lax.rem(me + n + n // 2 + step * (2 * (i % 2) - 1), n)
                pltpu.make_async_remote_copy(
                    src_ref=send.at[k1, to, cut],
                    dst_ref=recv.at[chunk, me],
                    send_sem=send_sem.at[k1],
                    recv_sem=recv_sem.at[chunk],
                    device_id={"chan": to},
                    device_id_type=pl.DeviceIdType.MESH,
                ).start()

    def exchange(chunk):
        return pltpu.make_async_remote_copy(
            src_ref=part.at[chunk, :, pl.ds(pl.multiple_of((1 - t) * half, half), half), :],
            dst_ref=other.at[chunk],
            send_sem=tm_send_sem.at[chunk],
            recv_sem=tm_recv_sem.at[chunk],
            device_id={"tm": 1 - t},
            device_id_type=pl.DeviceIdType.MESH,
        )

    def finish(chunk):
        exchange(chunk).wait_recv()
        own = part[chunk, :, pl.ds(pl.multiple_of(t * half, half), half), :]
        out_ref[chunk % split, :, chunk // split] = (own + other[chunk]) * (1.0 / (2 * specs))

    @pl.loop(0, chunks)
    def _(chunk):
        pltpu.make_async_copy(recv.at[chunk], recv.at[chunk], recv_sem.at[chunk]).wait()

        @pl.loop(0, pairs)
        def _(j):
            at = pl.multiple_of(j * 4 * inputs, 4 * inputs)
            turned = []
            for g in range(groups):
                block = recv[chunk, g * GROUP : (g + 1) * GROUP, pl.ds(at, 4 * inputs), :]
                block = block.reshape(GROUP * 4 * inputs, specs)
                turned.append(jnp.dot(perm_ref[...], block, preferred_element_type=jnp.float32).astype(jnp.bfloat16))
            run = GROUP * inputs
            for c in range(2):
                real = jnp.concatenate([x[2 * c * run : (2 * c + 1) * run] for x in turned], axis=0)
                imag = jnp.concatenate([x[(2 * c + 1) * run : (2 * c + 2) * run] for x in turned], axis=0)
                left = jnp.concatenate([real, imag], axis=1)
                right = jnp.concatenate([left, jnp.concatenate([-imag, real], axis=1)], axis=0)
                part[chunk, 2 * j + c] = lax.dot_general(left, right, NT, preferred_element_type=jnp.float32)

        exchange(chunk).start()

        @pl.when(chunk > 0)
        def _():
            finish(chunk - 1)

    finish(chunks - 1)

    @pl.when(t == 0)
    def _():
        halo.wait_send()

    @pl.loop(0, chunks)
    def _(chunk):
        exchange(chunk).wait_send()

    @pl.loop(0, RADIX)
    def _(k1):
        pltpu.make_async_copy(send.at[k1, 0 : n - 1], send.at[k1, 0 : n - 1], send_sem.at[k1]).wait()


def local_few(n, voltages):
    inputs = voltages.shape[1]
    specs = voltages.shape[2] // NCH
    tiles = NCH // LANES
    frame = tiles * inputs
    volts = voltages.reshape(2, inputs, specs * tiles, LANES).transpose(0, 2, 1, 3).reshape(2, specs * frame, LANES)
    high, low = make_dft(NCH)
    per = NCH // n // RADIX
    split = SPLIT if per % (2 * SPLIT) == 0 else 1
    chunks, each = RADIX * split, per // split
    total = n * inputs
    rows = each * 2 * inputs
    whole = pl.BlockSpec(memory_space=pltpu.VMEM)
    there = pl.BlockSpec(memory_space=pl.ANY)
    out = pl.pallas_call(
        functools.partial(kernel_few, n, inputs, specs),
        out_shape=jax.ShapeDtypeStruct((split, each, RADIX, total // 2, 2 * total), jnp.float32),
        in_specs=[there, whole, there, there, whole],
        out_specs=whole,
        scratch_shapes=[
            pltpu.VMEM((2, (specs + TAPS - 1) * frame, LANES), jnp.int32),
            pltpu.VMEM((RADIX, NCH // 2, NCH // 2), jnp.bfloat16),
            pltpu.VMEM((RADIX, NCH // 2, NCH // 2), jnp.bfloat16),
            pltpu.VMEM((2, BLOCK * tiles, LANES), jnp.float32),
            pltpu.VMEM((RADIX, inputs * specs, NCH // 2), jnp.bfloat16),
            pltpu.VMEM((RADIX, inputs * specs, NCH // 2), jnp.bfloat16),
            pltpu.VMEM((NCH // RADIX * 2 * inputs, specs), jnp.float32),
            pltpu.VMEM((RADIX, n, split * rows, specs), jnp.bfloat16),
            pltpu.VMEM((chunks, n, rows, specs), jnp.bfloat16),
            pltpu.VMEM((chunks, each, total, 2 * total), jnp.float32),
            pltpu.VMEM((chunks, each, total // 2, 2 * total), jnp.float32),
            pltpu.SemaphoreType.DMA((2,)),
            pltpu.SemaphoreType.DMA((2,)),
            pltpu.SemaphoreType.DMA,
            pltpu.SemaphoreType.DMA,
            pltpu.SemaphoreType.DMA((RADIX,)),
            pltpu.SemaphoreType.DMA((chunks,)),
            pltpu.SemaphoreType.DMA((chunks,)),
            pltpu.SemaphoreType.DMA((chunks,)),
        ],
        compiler_params=pltpu.CompilerParams(
            collective_id=0, has_side_effects=True, vmem_limit_bytes=60 * 1024 * 1024
        ),
    )(
        volts,
        jnp.asarray(make_taps(NCH).reshape(TAPS, tiles, LANES)),
        jnp.asarray(high),
        jnp.asarray(low),
        jnp.asarray(make_permutation(inputs)),
    )
    out = out.reshape(1, RADIX * per, total // 2, 2 * total)
    first = lax.broadcasted_iota(jnp.int32, (2, 1, 1, 1), 0) == 0
    return jnp.where(first, out[..., :total], out[..., total:])


def kernel(
    n,
    inputs,
    specs,
    volts_ref,
    taps_ref,
    high_ref,
    low_ref,
    out_ref,
    raw,
    high,
    low,
    filtered,
    y_high,
    y_low,
    send,
    recv,
    turned,
    part,
    other,
    result,
    load_sem,
    table_sem,
    halo_send_sem,
    halo_recv_sem,
    send_sem,
    recv_sem,
    tm_send_sem,
    tm_recv_sem,
    out_sem,
):
    me = lax.axis_index("chan")
    t = lax.axis_index("tm")
    sub = NCH // RADIX
    frame = NCH // LANES * inputs
    before = (TAPS - 1) * frame
    split = recv.shape[3]
    chunks = RADIX * split
    total = n * inputs
    half = total // 2

    barrier = pltpu.get_barrier_semaphore()

    @pl.loop(1, n)
    def _(i):
        pl.semaphore_signal(barrier, inc=1, device_id={"chan": lax.rem(me + i, n)}, device_id_type=pl.DeviceIdType.MESH)

    pl.semaphore_signal(barrier, inc=1, device_id={"tm": 1 - t}, device_id_type=pl.DeviceIdType.MESH)

    loads = [
        pltpu.make_async_copy(volts_ref.at[p], raw.at[p, before : before + specs * frame, :], load_sem.at[p])
        for p in range(2)
    ]
    tables = [
        pltpu.make_async_copy(high_ref, high, table_sem.at[0]),
        pltpu.make_async_copy(low_ref, low, table_sem.at[1]),
    ]
    for copy in loads + tables:
        copy.start()

    halo = pltpu.make_async_remote_copy(
        src_ref=volts_ref.at[:, specs * frame - before : specs * frame, :],
        dst_ref=raw.at[:, 0:before, :],
        send_sem=halo_send_sem,
        recv_sem=halo_recv_sem,
        device_id={"tm": 1 - t},
        device_id_type=pl.DeviceIdType.MESH,
    )
    pl.semaphore_wait(barrier, n)

    @pl.when(t == 0)
    def _():
        halo.start()
        raw[:, 0:before, :] = jnp.zeros((2, before, LANES), jnp.int32)

    for copy in loads:
        copy.wait()

    def transform(k1, rows, columns):
        mh, ml = high[k1, rows, :], low[k1, rows, :]
        yh, yl = y_high[k1, columns, :], y_low[k1, columns, :]
        value = lax.dot_general(mh, yh, NT, preferred_element_type=jnp.float32)
        value = value + lax.dot_general(mh, yl, NT, preferred_element_type=jnp.float32)
        return value + lax.dot_general(ml, yh, NT, preferred_element_type=jnp.float32)

    def to_partners(k1, cut, sem):
        pltpu.make_async_copy(send.at[(k1, me) + cut], recv.at[(k1, me) + cut], sem).start()

        @pl.loop(0, n - 1)
        def _(i):
            step = (i + 1) // 2
            to = lax.rem(me + n + n // 2 + step * (2 * (i % 2) - 1), n)
            pltpu.make_async_remote_copy(
                src_ref=send.at[(k1, to) + cut],
                dst_ref=recv.at[(k1, me) + cut],
                send_sem=send_sem.at[k1],
                recv_sem=sem,
                device_id={"chan": to},
                device_id_type=pl.DeviceIdType.MESH,
            ).start()

    for pair in range(inputs // 2):
        pick = range(2 * pair, 2 * pair + 2)

        @pl.loop(1, specs // BLOCK)
        def _(b):
            for a in pick:
                filter_block(b, a, inputs, specs, raw, taps_ref, filtered, y_high, y_low)

        if pair == 0:

            @pl.when(t == 1)
            def _():
                halo.wait_recv()

        for a in pick:
            filter_block(0, a, inputs, specs, raw, taps_ref, filtered, y_high, y_low)
        if pair == 0:
            for copy in tables:
                copy.wait()
        value = transform(0, slice(0, 2 * sub), slice(2 * pair * specs, 2 * (pair + 1) * specs))
        for i, a in enumerate(pick):
            send[0, :, a] = value[:, i * specs : (i + 1) * specs].astype(jnp.bfloat16).reshape(n, split, 16, specs)
        to_partners(0, (slice(2 * pair, 2 * pair + 2),), recv_sem.at[0])

    @pl.loop(1, RADIX)
    def _(k1):
        for p in range(2):
            value = transform(k1, slice(p * sub, (p + 1) * sub), slice(0, inputs * specs))
            for a in range(inputs):
                mine = value[:, a * specs : (a + 1) * specs].astype(jnp.bfloat16)
                send[k1, p * n // 2 : (p + 1) * n // 2, a] = mine.reshape(n // 2, split, 16, specs)
        for h in range(split):
            to_partners(k1, (slice(0, inputs), h), recv_sem.at[k1 * split + h])

    def exchange(chunk):
        return pltpu.make_async_remote_copy(
            src_ref=part.at[chunk, :, pl.ds(pl.multiple_of((1 - t) * half, half), half), :],
            dst_ref=other.at[chunk],
            send_sem=tm_send_sem.at[chunk],
            recv_sem=tm_recv_sem.at[chunk],
            device_id={"tm": 1 - t},
            device_id_type=pl.DeviceIdType.MESH,
        )

    def store(chunk):
        return pltpu.make_async_copy(
            result.at[chunk], out_ref.at[:, chunk % split, :, chunk // split], out_sem.at[chunk]
        )

    def finish(chunk):
        exchange(chunk).wait_recv()
        own = part[chunk, :, pl.ds(pl.multiple_of(t * half, half), half), :]
        value = (own + other[chunk]) * (1.0 / (2 * specs))
        result[chunk, 0] = value[:, :, :total]
        result[chunk, 1] = value[:, :, total:]
        store(chunk).start()

    @pl.loop(0, chunks)
    def _(chunk):
        k1, h = chunk // split, chunk % split

        @pl.when(chunk == 0)
        def _():
            pltpu.make_async_copy(recv.at[0], recv.at[0], recv_sem.at[0]).wait()

        @pl.when(chunk >= split)
        def _():
            came = recv.at[k1, :, :, h]
            pltpu.make_async_copy(came, came, recv_sem.at[chunk]).wait()

        turned[...] = recv[k1, :, :, h].astype(jnp.float32).reshape(total * 16, specs)
        for c in range(8):
            real = turned[pl.ds(c, total, 16), :].astype(jnp.bfloat16)
            imag = turned[pl.ds(8 + c, total, 16), :].astype(jnp.bfloat16)
            left = jnp.concatenate([real, imag], axis=1)
            right = jnp.concatenate([left, jnp.concatenate([-imag, real], axis=1)], axis=0)
            part[chunk, c] = lax.dot_general(left, right, NT, preferred_element_type=jnp.float32)

        exchange(chunk).start()

        @pl.when(chunk > 0)
        def _():
            finish(chunk - 1)

    finish(chunks - 1)

    @pl.when(t == 0)
    def _():
        halo.wait_send()

    @pl.loop(0, chunks)
    def _(chunk):
        exchange(chunk).wait_send()
        store(chunk).wait()

    @pl.loop(0, RADIX)
    def _(k1):
        pltpu.make_async_copy(send.at[k1, 0 : n - 1], send.at[k1, 0 : n - 1], send_sem.at[k1]).wait()


def local(n, voltages):
    inputs = voltages.shape[1]
    specs = voltages.shape[2] // NCH
    per = NCH // n // RADIX
    if per % 8:
        return local_few(n, voltages)
    tiles = NCH // LANES
    frame = tiles * inputs
    volts = voltages.reshape(2, inputs, specs * tiles, LANES).transpose(0, 2, 1, 3).reshape(2, specs * frame, LANES)
    high, low = make_dft(NCH)
    split = per // 8
    chunks = RADIX * split
    total = n * inputs

    def tiled(m):
        return m.reshape(RADIX, 2, NCH // RADIX // 8, 8, NCH // 2).transpose(0, 2, 1, 3, 4).reshape(m.shape)

    whole = pl.BlockSpec(memory_space=pltpu.VMEM)
    there = pl.BlockSpec(memory_space=pl.ANY)
    out = pl.pallas_call(
        functools.partial(kernel, n, inputs, specs),
        out_shape=jax.ShapeDtypeStruct((2, split, 8, RADIX, total // 2, total), jnp.float32),
        in_specs=[there, whole, there, there],
        out_specs=there,
        scratch_shapes=[
            pltpu.VMEM((2, (specs + TAPS - 1) * frame, LANES), jnp.int32),
            pltpu.VMEM((RADIX, NCH // 2, NCH // 2), jnp.bfloat16),
            pltpu.VMEM((RADIX, NCH // 2, NCH // 2), jnp.bfloat16),
            pltpu.VMEM((2, BLOCK * tiles, LANES), jnp.float32),
            pltpu.VMEM((RADIX, inputs * specs, NCH // 2), jnp.bfloat16),
            pltpu.VMEM((RADIX, inputs * specs, NCH // 2), jnp.bfloat16),
            pltpu.VMEM((RADIX, n, inputs, split, 16, specs), jnp.bfloat16),
            pltpu.VMEM((RADIX, n, inputs, split, 16, specs), jnp.bfloat16),
            pltpu.VMEM((total * 16, specs), jnp.float32),
            pltpu.VMEM((chunks, 8, total, 2 * total), jnp.float32),
            pltpu.VMEM((chunks, 8, total // 2, 2 * total), jnp.float32),
            pltpu.VMEM((chunks, 2, 8, total // 2, total), jnp.float32),
            pltpu.SemaphoreType.DMA((2,)),
            pltpu.SemaphoreType.DMA((2,)),
            pltpu.SemaphoreType.DMA,
            pltpu.SemaphoreType.DMA,
            pltpu.SemaphoreType.DMA((RADIX,)),
            pltpu.SemaphoreType.DMA((chunks,)),
            pltpu.SemaphoreType.DMA((chunks,)),
            pltpu.SemaphoreType.DMA((chunks,)),
            pltpu.SemaphoreType.DMA((chunks,)),
        ],
        compiler_params=pltpu.CompilerParams(
            collective_id=0, has_side_effects=True, vmem_limit_bytes=60 * 1024 * 1024
        ),
    )(
        volts,
        jnp.asarray(make_taps(NCH).reshape(TAPS, tiles, LANES)),
        jnp.asarray(tiled(high)),
        jnp.asarray(tiled(low)),
    )
    return out.reshape(2, RADIX * per, total // 2, total)


def solution(mesh):
    placed = (P(None, "chan", "tm"),)
    return jax.shard_map(
        functools.partial(local, mesh.shape["chan"]),
        mesh=mesh,
        in_specs=placed,
        out_specs=P(None, "chan", "tm", None),
        check_vma=False,
    )
```

```python
import functools

import jax
import jax.numpy as jnp
import ml_dtypes
import numpy as np
from jax import lax
from jax.experimental import pallas as pl
from jax.experimental.pallas import tpu as pltpu
from jax.sharding import PartitionSpec as P

NCH = 1024
TAPS = 4
RADIX = 4
GROUP = 16
LANES = 128
BLOCK = 16
SPLIT = 2
NT = (((1,), (1,)), ((), ()))


def make_taps(nch):
    k = np.arange(TAPS * nch, dtype=np.float64)
    x = (k - 2.0 * nch + 0.5) / nch
    window = 0.54 - 0.46 * np.cos(2.0 * np.pi * (k + 0.5) / (TAPS * nch))
    return (np.sinc(x) * window).reshape(TAPS, nch).astype(np.float32)


def make_dft(nch):
    sub = nch // RADIX
    n = np.arange(sub)
    highs, lows = [], []
    for r in range(RADIX):
        k = RADIX * np.arange(sub) + r
        angle = (k[:, None] * n[None, :] % nch) * (2.0 * np.pi / nch)
        c, s = np.cos(angle), np.sin(angle)
        m = np.block([[c, s], [-s, c]]) * (0.25 / np.sqrt(nch))
        high = m.astype(np.float32).astype(ml_dtypes.bfloat16)
        low = (m - high.astype(np.float64)).astype(np.float32).astype(ml_dtypes.bfloat16)
        highs.append(high)
        lows.append(low)
    return np.stack(highs), np.stack(lows)


def make_permutation(local_inputs):
    size = GROUP * 4 * local_inputs
    order = np.arange(size).reshape(GROUP, 2, 2, local_inputs).transpose(1, 2, 0, 3).reshape(-1)
    perm = np.zeros((size, size), np.float32)
    perm[np.arange(size), order] = 1.0
    return perm.astype(ml_dtypes.bfloat16)


def filter_block(b, a, inputs, specs, raw, taps_ref, filtered, y_high, y_low):
    sub = NCH // RADIX
    tiles = NCH // LANES
    frame = tiles * inputs
    at = b * BLOCK
    for p in range(2):
        frames = raw[p, pl.ds(at * frame + a, (BLOCK + TAPS - 1) * tiles, inputs), :].astype(jnp.float32)
        frames = frames.reshape(BLOCK + TAPS - 1, tiles, LANES)
        value = taps_ref[0] * frames[0:BLOCK]
        for step in range(1, TAPS):
            value = value + taps_ref[step] * frames[step : step + BLOCK]
        filtered[p] = value.reshape(BLOCK * tiles, LANES)
    quarter = tiles // RADIX
    place = pl.ds(pl.multiple_of(a * specs + at, BLOCK), BLOCK)
    for h in range(quarter):
        r, im = [[filtered[p, pl.ds(q * quarter + h, BLOCK, tiles), :] for q in range(RADIX)] for p in range(2)]
        er, orr, dr, gr = r[0] + r[2], r[1] + r[3], r[0] - r[2], r[1] - r[3]
        ei, oi, di, gi = im[0] + im[2], im[1] + im[3], im[0] - im[2], im[1] - im[3]
        parts = [(er + orr, ei + oi), (dr + gi, di - gr), (er - orr, ei - oi), (dr - gi, di + gr)]
        for k1 in range(RADIX):
            for p in range(2):
                value = parts[k1][p]
                top = value.astype(jnp.bfloat16)
                lanes = slice(p * sub + h * LANES, p * sub + (h + 1) * LANES)
                y_high[k1, place, lanes] = top
                y_low[k1, place, lanes] = (value - top.astype(jnp.float32)).astype(jnp.bfloat16)


def kernel_few(
    n,
    inputs,
    specs,
    volts_ref,
    taps_ref,
    high_ref,
    low_ref,
    perm_ref,
    out_ref,
    raw,
    high,
    low,
    filtered,
    y_high,
    y_low,
    spread,
    send,
    recv,
    part,
    other,
    load_sem,
    table_sem,
    halo_send_sem,
    halo_recv_sem,
    send_sem,
    recv_sem,
    tm_send_sem,
    tm_recv_sem,
):
    me = lax.axis_index("chan")
    t = lax.axis_index("tm")
    sub = NCH // RADIX
    tiles = NCH // LANES
    frame = tiles * inputs
    before = (TAPS - 1) * frame
    chunks = recv.shape[0]
    split = chunks // RADIX
    rows = recv.shape[2]
    pairs = rows // (4 * inputs)
    groups = n // GROUP
    half = n * inputs // 2

    barrier = pltpu.get_barrier_semaphore()

    @pl.loop(1, n)
    def _(i):
        pl.semaphore_signal(barrier, inc=1, device_id={"chan": lax.rem(me + i, n)}, device_id_type=pl.DeviceIdType.MESH)

    pl.semaphore_signal(barrier, inc=1, device_id={"tm": 1 - t}, device_id_type=pl.DeviceIdType.MESH)

    loads = [
        pltpu.make_async_copy(volts_ref.at[p], raw.at[p, before : before + specs * frame, :], load_sem.at[p])
        for p in range(2)
    ]
    tables = [
        pltpu.make_async_copy(high_ref, high, table_sem.at[0]),
        pltpu.make_async_copy(low_ref, low, table_sem.at[1]),
    ]
    for copy in loads + tables:
        copy.start()

    halo = pltpu.make_async_remote_copy(
        src_ref=volts_ref.at[:, specs * frame - before : specs * frame, :],
        dst_ref=raw.at[:, 0:before, :],
        send_sem=halo_send_sem,
        recv_sem=halo_recv_sem,
        device_id={"tm": 1 - t},
        device_id_type=pl.DeviceIdType.MESH,
    )
    pl.semaphore_wait(barrier, n)

    @pl.when(t == 0)
    def _():
        halo.start()
        raw[:, 0:before, :] = jnp.zeros((2, before, LANES), jnp.int32)

    for copy in loads:
        copy.wait()

    @pl.loop(1, specs // BLOCK)
    def _(b):
        for a in range(inputs):
            filter_block(b, a, inputs, specs, raw, taps_ref, filtered, y_high, y_low)

    @pl.when(t == 1)
    def _():
        halo.wait_recv()

    for a in range(inputs):
        filter_block(0, a, inputs, specs, raw, taps_ref, filtered, y_high, y_low)

    for copy in tables:
        copy.wait()

    @pl.loop(0, RADIX)
    def _(k1):
        for p in range(2):
            mine = slice(p * sub, (p + 1) * sub)
            mh, ml = high[k1, mine, :], low[k1, mine, :]
            yh, yl = y_high[k1], y_low[k1]
            value = lax.dot_general(mh, yh, NT, preferred_element_type=jnp.float32)
            value = value + lax.dot_general(mh, yl, NT, preferred_element_type=jnp.float32)
            value = value + lax.dot_general(ml, yh, NT, preferred_element_type=jnp.float32)
            for a in range(inputs):
                spread[pl.ds(p * inputs + a, sub, 2 * inputs), :] = value[:, a * specs : (a + 1) * specs]
        send[k1] = spread[...].astype(jnp.bfloat16).reshape(n, split * rows, specs)
        for h in range(split):
            chunk = k1 * split + h
            cut = pl.ds(h * rows, rows)
            pltpu.make_async_copy(send.at[k1, me, cut], recv.at[chunk, me], recv_sem.at[chunk]).start()

            @pl.loop(0, n - 1)
            def _(i):
                step = (i + 1) // 2
                to = lax.rem(me + n + n // 2 + step * (2 * (i % 2) - 1), n)
                pltpu.make_async_remote_copy(
                    src_ref=send.at[k1, to, cut],
                    dst_ref=recv.at[chunk, me],
                    send_sem=send_sem.at[k1],
                    recv_sem=recv_sem.at[chunk],
                    device_id={"chan": to},
                    device_id_type=pl.DeviceIdType.MESH,
                ).start()

    def exchange(chunk):
        return pltpu.make_async_remote_copy(
            src_ref=part.at[chunk, :, pl.ds(pl.multiple_of((1 - t) * half, half), half), :],
            dst_ref=other.at[chunk],
            send_sem=tm_send_sem.at[chunk],
            recv_sem=tm_recv_sem.at[chunk],
            device_id={"tm": 1 - t},
            device_id_type=pl.DeviceIdType.MESH,
        )

    def finish(chunk):
        exchange(chunk).wait_recv()
        own = part[chunk, :, pl.ds(pl.multiple_of(t * half, half), half), :]
        out_ref[chunk % split, :, chunk // split] = (own + other[chunk]) * (1.0 / (2 * specs))

    @pl.loop(0, chunks)
    def _(chunk):
        pltpu.make_async_copy(recv.at[chunk], recv.at[chunk], recv_sem.at[chunk]).wait()

        @pl.loop(0, pairs)
        def _(j):
            at = pl.multiple_of(j * 4 * inputs, 4 * inputs)
            turned = []
            for g in range(groups):
                block = recv[chunk, g * GROUP : (g + 1) * GROUP, pl.ds(at, 4 * inputs), :]
                block = block.reshape(GROUP * 4 * inputs, specs)
                turned.append(jnp.dot(perm_ref[...], block, preferred_element_type=jnp.float32).astype(jnp.bfloat16))
            run = GROUP * inputs
            for c in range(2):
                real = jnp.concatenate([x[2 * c * run : (2 * c + 1) * run] for x in turned], axis=0)
                imag = jnp.concatenate([x[(2 * c + 1) * run : (2 * c + 2) * run] for x in turned], axis=0)
                left = jnp.concatenate([real, imag], axis=1)
                right = jnp.concatenate([left, jnp.concatenate([-imag, real], axis=1)], axis=0)
                part[chunk, 2 * j + c] = lax.dot_general(left, right, NT, preferred_element_type=jnp.float32)

        exchange(chunk).start()

        @pl.when(chunk > 0)
        def _():
            finish(chunk - 1)

    finish(chunks - 1)

    @pl.when(t == 0)
    def _():
        halo.wait_send()

    @pl.loop(0, chunks)
    def _(chunk):
        exchange(chunk).wait_send()

    @pl.loop(0, RADIX)
    def _(k1):
        pltpu.make_async_copy(send.at[k1, 0 : n - 1], send.at[k1, 0 : n - 1], send_sem.at[k1]).wait()


def local_few(n, voltages):
    inputs = voltages.shape[1]
    specs = voltages.shape[2] // NCH
    tiles = NCH // LANES
    frame = tiles * inputs
    volts = voltages.reshape(2, inputs, specs * tiles, LANES).transpose(0, 2, 1, 3).reshape(2, specs * frame, LANES)
    high, low = make_dft(NCH)
    per = NCH // n // RADIX
    split = SPLIT if per % (2 * SPLIT) == 0 else 1
    chunks, each = RADIX * split, per // split
    total = n * inputs
    rows = each * 2 * inputs
    whole = pl.BlockSpec(memory_space=pltpu.VMEM)
    there = pl.BlockSpec(memory_space=pl.ANY)
    out = pl.pallas_call(
        functools.partial(kernel_few, n, inputs, specs),
        out_shape=jax.ShapeDtypeStruct((split, each, RADIX, total // 2, 2 * total), jnp.float32),
        in_specs=[there, whole, there, there, whole],
        out_specs=whole,
        scratch_shapes=[
            pltpu.VMEM((2, (specs + TAPS - 1) * frame, LANES), jnp.int32),
            pltpu.VMEM((RADIX, NCH // 2, NCH // 2), jnp.bfloat16),
            pltpu.VMEM((RADIX, NCH // 2, NCH // 2), jnp.bfloat16),
            pltpu.VMEM((2, BLOCK * tiles, LANES), jnp.float32),
            pltpu.VMEM((RADIX, inputs * specs, NCH // 2), jnp.bfloat16),
            pltpu.VMEM((RADIX, inputs * specs, NCH // 2), jnp.bfloat16),
            pltpu.VMEM((NCH // RADIX * 2 * inputs, specs), jnp.float32),
            pltpu.VMEM((RADIX, n, split * rows, specs), jnp.bfloat16),
            pltpu.VMEM((chunks, n, rows, specs), jnp.bfloat16),
            pltpu.VMEM((chunks, each, total, 2 * total), jnp.float32),
            pltpu.VMEM((chunks, each, total // 2, 2 * total), jnp.float32),
            pltpu.SemaphoreType.DMA((2,)),
            pltpu.SemaphoreType.DMA((2,)),
            pltpu.SemaphoreType.DMA,
            pltpu.SemaphoreType.DMA,
            pltpu.SemaphoreType.DMA((RADIX,)),
            pltpu.SemaphoreType.DMA((chunks,)),
            pltpu.SemaphoreType.DMA((chunks,)),
            pltpu.SemaphoreType.DMA((chunks,)),
        ],
        compiler_params=pltpu.CompilerParams(
            collective_id=0, has_side_effects=True, vmem_limit_bytes=60 * 1024 * 1024
        ),
    )(
        volts,
        jnp.asarray(make_taps(NCH).reshape(TAPS, tiles, LANES)),
        jnp.asarray(high),
        jnp.asarray(low),
        jnp.asarray(make_permutation(inputs)),
    )
    out = out.reshape(1, RADIX * per, total // 2, 2 * total)
    first = lax.broadcasted_iota(jnp.int32, (2, 1, 1, 1), 0) == 0
    return jnp.where(first, out[..., :total], out[..., total:])


def kernel(
    n,
    inputs,
    specs,
    volts_ref,
    taps_ref,
    high_ref,
    low_ref,
    out_ref,
    raw,
    high,
    low,
    filtered,
    y_high,
    y_low,
    send,
    recv,
    turned,
    part,
    other,
    result,
    load_sem,
    table_sem,
    halo_send_sem,
    halo_recv_sem,
    send_sem,
    recv_sem,
    tm_send_sem,
    tm_recv_sem,
    out_sem,
):
    me = lax.axis_index("chan")
    t = lax.axis_index("tm")
    sub = NCH // RADIX
    frame = NCH // LANES * inputs
    before = (TAPS - 1) * frame
    split = recv.shape[3]
    chunks = RADIX * split
    total = n * inputs
    half = total // 2

    barrier = pltpu.get_barrier_semaphore()

    @pl.loop(1, n)
    def _(i):
        pl.semaphore_signal(barrier, inc=1, device_id={"chan": lax.rem(me + i, n)}, device_id_type=pl.DeviceIdType.MESH)

    pl.semaphore_signal(barrier, inc=1, device_id={"tm": 1 - t}, device_id_type=pl.DeviceIdType.MESH)

    loads = [
        pltpu.make_async_copy(volts_ref.at[p], raw.at[p, before : before + specs * frame, :], load_sem.at[p])
        for p in range(2)
    ]
    tables = [
        pltpu.make_async_copy(high_ref, high, table_sem.at[0]),
        pltpu.make_async_copy(low_ref, low, table_sem.at[1]),
    ]
    for copy in loads:
        copy.start()

    halo = pltpu.make_async_remote_copy(
        src_ref=volts_ref.at[:, specs * frame - before : specs * frame, :],
        dst_ref=raw.at[:, 0:before, :],
        send_sem=halo_send_sem,
        recv_sem=halo_recv_sem,
        device_id={"tm": 1 - t},
        device_id_type=pl.DeviceIdType.MESH,
    )
    pl.semaphore_wait(barrier, n)

    @pl.when(t == 0)
    def _():
        halo.start()
        raw[:, 0:before, :] = jnp.zeros((2, before, LANES), jnp.int32)

    for copy in loads:
        copy.wait()
    for copy in tables:
        copy.start()

    def transform(k1, rows, columns):
        mh, ml = high[k1, rows, :], low[k1, rows, :]
        yh, yl = y_high[k1, columns, :], y_low[k1, columns, :]
        value = lax.dot_general(mh, yh, NT, preferred_element_type=jnp.float32)
        value = value + lax.dot_general(mh, yl, NT, preferred_element_type=jnp.float32)
        return value + lax.dot_general(ml, yh, NT, preferred_element_type=jnp.float32)

    def to_partners(k1, cut, sem):
        pltpu.make_async_copy(send.at[(k1, me) + cut], recv.at[(k1, me) + cut], sem).start()

        @pl.loop(0, n - 1)
        def _(i):
            step = (i + 1) // 2
            to = lax.rem(me + n + n // 2 + step * (2 * (i % 2) - 1), n)
            pltpu.make_async_remote_copy(
                src_ref=send.at[(k1, to) + cut],
                dst_ref=recv.at[(k1, me) + cut],
                send_sem=send_sem.at[k1],
                recv_sem=sem,
                device_id={"chan": to},
                device_id_type=pl.DeviceIdType.MESH,
            ).start()

    for pick in [range(0, 1), range(1, 2)] + [range(a, a + 2) for a in range(2, inputs, 2)]:

        @pl.loop(1, specs // BLOCK)
        def _(b):
            for a in pick:
                filter_block(b, a, inputs, specs, raw, taps_ref, filtered, y_high, y_low)

        if 0 in pick:

            @pl.when(t == 1)
            def _():
                halo.wait_recv()

        for a in pick:
            filter_block(0, a, inputs, specs, raw, taps_ref, filtered, y_high, y_low)
        if 0 in pick:
            for copy in tables:
                copy.wait()
        value = transform(0, slice(0, 2 * sub), slice(pick.start * specs, pick.stop * specs))
        for i, a in enumerate(pick):
            send[0, :, a] = value[:, i * specs : (i + 1) * specs].astype(jnp.bfloat16).reshape(n, split, 16, specs)
        to_partners(0, (slice(pick.start, pick.stop),), recv_sem.at[0])

    @pl.loop(1, RADIX)
    def _(k1):
        for p in range(2):
            value = transform(k1, slice(p * sub, (p + 1) * sub), slice(0, inputs * specs))
            for a in range(inputs):
                mine = value[:, a * specs : (a + 1) * specs].astype(jnp.bfloat16)
                send[k1, p * n // 2 : (p + 1) * n // 2, a] = mine.reshape(n // 2, split, 16, specs)
        for h in range(split):
            to_partners(k1, (slice(0, inputs), h), recv_sem.at[k1 * split + h])

    def exchange(chunk, q):
        return pltpu.make_async_remote_copy(
            src_ref=part.at[chunk, 4 * q : 4 * q + 4, pl.ds(pl.multiple_of((1 - t) * half, half), half), :],
            dst_ref=other.at[chunk, 4 * q : 4 * q + 4],
            send_sem=tm_send_sem.at[chunk, q],
            recv_sem=tm_recv_sem.at[chunk, q],
            device_id={"tm": 1 - t},
            device_id_type=pl.DeviceIdType.MESH,
        )

    def store(chunk, q):
        return pltpu.make_async_copy(
            result.at[chunk, :, 4 * q : 4 * q + 4],
            out_ref.at[:, chunk % split, 4 * q : 4 * q + 4, chunk // split],
            out_sem.at[chunk, q],
        )

    def finish(chunk):
        for q in range(2):
            exchange(chunk, q).wait_recv()
            own = part[chunk, 4 * q : 4 * q + 4, pl.ds(pl.multiple_of(t * half, half), half), :]
            value = (own + other[chunk, 4 * q : 4 * q + 4]) * (1.0 / (2 * specs))
            result[chunk, 0, 4 * q : 4 * q + 4] = value[:, :, :total]
            result[chunk, 1, 4 * q : 4 * q + 4] = value[:, :, total:]
            store(chunk, q).start()

    @pl.loop(0, chunks)
    def _(chunk):
        k1, h = chunk // split, chunk % split

        @pl.when(chunk == 0)
        def _():
            pltpu.make_async_copy(recv.at[0], recv.at[0], recv_sem.at[0]).wait()

        @pl.when(chunk >= split)
        def _():
            came = recv.at[k1, :, :, h]
            pltpu.make_async_copy(came, came, recv_sem.at[chunk]).wait()

        turned[...] = recv[k1, :, :, h].astype(jnp.float32).reshape(total * 16, specs)
        for c in range(8):
            real = turned[pl.ds(c, total, 16), :].astype(jnp.bfloat16)
            imag = turned[pl.ds(8 + c, total, 16), :].astype(jnp.bfloat16)
            left = jnp.concatenate([real, imag], axis=1)
            right = jnp.concatenate([left, jnp.concatenate([-imag, real], axis=1)], axis=0)
            part[chunk, c] = lax.dot_general(left, right, NT, preferred_element_type=jnp.float32)
            if c % 4 == 3:
                exchange(chunk, c // 4).start()

        @pl.when(chunk > 0)
        def _():
            finish(chunk - 1)

    finish(chunks - 1)

    @pl.when(t == 0)
    def _():
        halo.wait_send()

    @pl.loop(0, chunks)
    def _(chunk):
        for q in range(2):
            exchange(chunk, q).wait_send()
            store(chunk, q).wait()

    @pl.loop(0, RADIX)
    def _(k1):
        pltpu.make_async_copy(send.at[k1, 0 : n - 1], send.at[k1, 0 : n - 1], send_sem.at[k1]).wait()


def local(n, voltages):
    inputs = voltages.shape[1]
    specs = voltages.shape[2] // NCH
    per = NCH // n // RADIX
    if per % 8:
        return local_few(n, voltages)
    tiles = NCH // LANES
    frame = tiles * inputs
    volts = voltages.reshape(2, inputs, specs * tiles, LANES).transpose(0, 2, 1, 3).reshape(2, specs * frame, LANES)
    high, low = make_dft(NCH)
    split = per // 8
    chunks = RADIX * split
    total = n * inputs

    def tiled(m):
        return m.reshape(RADIX, 2, NCH // RADIX // 8, 8, NCH // 2).transpose(0, 2, 1, 3, 4).reshape(m.shape)

    whole = pl.BlockSpec(memory_space=pltpu.VMEM)
    there = pl.BlockSpec(memory_space=pltpu.HBM)
    out = pl.pallas_call(
        functools.partial(kernel, n, inputs, specs),
        out_shape=jax.ShapeDtypeStruct((2, split, 8, RADIX, total // 2, total), jnp.float32),
        in_specs=[there, whole, there, there],
        out_specs=pl.BlockSpec(memory_space=pl.ANY),
        scratch_shapes=[
            pltpu.VMEM((2, (specs + TAPS - 1) * frame, LANES), jnp.int32),
            pltpu.VMEM((RADIX, NCH // 2, NCH // 2), jnp.bfloat16),
            pltpu.VMEM((RADIX, NCH // 2, NCH // 2), jnp.bfloat16),
            pltpu.VMEM((2, BLOCK * tiles, LANES), jnp.float32),
            pltpu.VMEM((RADIX, inputs * specs, NCH // 2), jnp.bfloat16),
            pltpu.VMEM((RADIX, inputs * specs, NCH // 2), jnp.bfloat16),
            pltpu.VMEM((RADIX, n, inputs, split, 16, specs), jnp.bfloat16),
            pltpu.VMEM((RADIX, n, inputs, split, 16, specs), jnp.bfloat16),
            pltpu.VMEM((total * 16, specs), jnp.float32),
            pltpu.VMEM((chunks, 8, total, 2 * total), jnp.float32),
            pltpu.VMEM((chunks, 8, total // 2, 2 * total), jnp.float32),
            pltpu.VMEM((chunks, 2, 8, total // 2, total), jnp.float32),
            pltpu.SemaphoreType.DMA((2,)),
            pltpu.SemaphoreType.DMA((2,)),
            pltpu.SemaphoreType.DMA,
            pltpu.SemaphoreType.DMA,
            pltpu.SemaphoreType.DMA((RADIX,)),
            pltpu.SemaphoreType.DMA((chunks,)),
            pltpu.SemaphoreType.DMA((chunks, 2)),
            pltpu.SemaphoreType.DMA((chunks, 2)),
            pltpu.SemaphoreType.DMA((chunks, 2)),
        ],
        compiler_params=pltpu.CompilerParams(
            collective_id=0, has_side_effects=True, vmem_limit_bytes=(44 if total <= 64 else 60) * 1024 * 1024
        ),
    )(
        volts,
        jnp.asarray(make_taps(NCH).reshape(TAPS, tiles, LANES)),
        jnp.asarray(tiled(high)),
        jnp.asarray(tiled(low)),
    )
    return out.reshape(2, RADIX * per, total // 2, total)


def solution(mesh):
    placed = (P(None, "chan", "tm"),)
    return jax.shard_map(
        functools.partial(local, mesh.shape["chan"]),
        mesh=mesh,
        in_specs=placed,
        out_specs=P(None, "chan", "tm", None),
        check_vma=False,
    )
```

```python
import functools

import jax
import jax.numpy as jnp
import ml_dtypes
import numpy as np
from jax import lax
from jax.experimental import pallas as pl
from jax.experimental.pallas import tpu as pltpu
from jax.sharding import PartitionSpec as P

NCH = 1024
TAPS = 4
RADIX = 4
GROUP = 16
LANES = 128
BLOCK = 16
SPLIT = 2
LOADS = 4
VMEM = 50
NT = (((1,), (1,)), ((), ()))


def make_taps(nch):
    k = np.arange(TAPS * nch, dtype=np.float64)
    x = (k - 2.0 * nch + 0.5) / nch
    window = 0.54 - 0.46 * np.cos(2.0 * np.pi * (k + 0.5) / (TAPS * nch))
    return (np.sinc(x) * window).reshape(TAPS, nch).astype(np.float32)


def make_dft(nch):
    sub = nch // RADIX
    n = np.arange(sub)
    highs, lows = [], []
    for r in range(RADIX):
        k = RADIX * np.arange(sub) + r
        angle = (k[:, None] * n[None, :] % nch) * (2.0 * np.pi / nch)
        c, s = np.cos(angle), np.sin(angle)
        m = np.block([[c, s], [-s, c]]) * (0.25 / np.sqrt(nch))
        high = m.astype(np.float32).astype(ml_dtypes.bfloat16)
        low = (m - high.astype(np.float64)).astype(np.float32).astype(ml_dtypes.bfloat16)
        highs.append(high)
        lows.append(low)
    return np.stack(highs), np.stack(lows)


def make_permutation(local_inputs):
    size = GROUP * 4 * local_inputs
    order = np.arange(size).reshape(GROUP, 2, 2, local_inputs).transpose(1, 2, 0, 3).reshape(-1)
    perm = np.zeros((size, size), np.float32)
    perm[np.arange(size), order] = 1.0
    return perm.astype(ml_dtypes.bfloat16)


def filter_block(b, a, inputs, specs, raw, taps_ref, filtered, y_high, y_low):
    sub = NCH // RADIX
    tiles = NCH // LANES
    frame = tiles * inputs
    at = b * BLOCK
    for p in range(2):
        frames = raw[p, pl.ds(at * frame + a, (BLOCK + TAPS - 1) * tiles, inputs), :].astype(jnp.float32)
        frames = frames.reshape(BLOCK + TAPS - 1, tiles, LANES)
        value = taps_ref[0] * frames[0:BLOCK]
        for step in range(1, TAPS):
            value = value + taps_ref[step] * frames[step : step + BLOCK]
        filtered[p] = value.reshape(BLOCK * tiles, LANES)
    quarter = tiles // RADIX
    place = pl.ds(pl.multiple_of(a * specs + at, BLOCK), BLOCK)
    for h in range(quarter):
        r, im = [[filtered[p, pl.ds(q * quarter + h, BLOCK, tiles), :] for q in range(RADIX)] for p in range(2)]
        er, orr, dr, gr = r[0] + r[2], r[1] + r[3], r[0] - r[2], r[1] - r[3]
        ei, oi, di, gi = im[0] + im[2], im[1] + im[3], im[0] - im[2], im[1] - im[3]
        parts = [(er + orr, ei + oi), (dr + gi, di - gr), (er - orr, ei - oi), (dr - gi, di + gr)]
        for k1 in range(RADIX):
            for p in range(2):
                value = parts[k1][p]
                top = value.astype(jnp.bfloat16)
                lanes = slice(p * sub + h * LANES, p * sub + (h + 1) * LANES)
                y_high[k1, place, lanes] = top
                y_low[k1, place, lanes] = (value - top.astype(jnp.float32)).astype(jnp.bfloat16)


def kernel_few(
    n,
    inputs,
    specs,
    volts_ref,
    taps_ref,
    high_ref,
    low_ref,
    perm_ref,
    out_ref,
    raw,
    high,
    low,
    filtered,
    y_high,
    y_low,
    spread,
    send,
    recv,
    part,
    other,
    load_sem,
    table_sem,
    halo_send_sem,
    halo_recv_sem,
    send_sem,
    recv_sem,
    tm_send_sem,
    tm_recv_sem,
):
    me = lax.axis_index("chan")
    t = lax.axis_index("tm")
    sub = NCH // RADIX
    tiles = NCH // LANES
    frame = tiles * inputs
    before = (TAPS - 1) * frame
    chunks = recv.shape[0]
    split = chunks // RADIX
    rows = recv.shape[2]
    pairs = rows // (4 * inputs)
    groups = n // GROUP
    half = n * inputs // 2

    barrier = pltpu.get_barrier_semaphore()

    @pl.loop(1, n)
    def _(i):
        pl.semaphore_signal(barrier, inc=1, device_id={"chan": lax.rem(me + i, n)}, device_id_type=pl.DeviceIdType.MESH)

    pl.semaphore_signal(barrier, inc=1, device_id={"tm": 1 - t}, device_id_type=pl.DeviceIdType.MESH)

    loads = [
        pltpu.make_async_copy(volts_ref.at[p], raw.at[p, before : before + specs * frame, :], load_sem.at[p])
        for p in range(2)
    ]
    tables = [
        pltpu.make_async_copy(high_ref, high, table_sem.at[0]),
        pltpu.make_async_copy(low_ref, low, table_sem.at[1]),
    ]
    for copy in loads + tables:
        copy.start()

    halo = pltpu.make_async_remote_copy(
        src_ref=volts_ref.at[:, specs * frame - before : specs * frame, :],
        dst_ref=raw.at[:, 0:before, :],
        send_sem=halo_send_sem,
        recv_sem=halo_recv_sem,
        device_id={"tm": 1 - t},
        device_id_type=pl.DeviceIdType.MESH,
    )
    pl.semaphore_wait(barrier, n)

    @pl.when(t == 0)
    def _():
        halo.start()
        raw[:, 0:before, :] = jnp.zeros((2, before, LANES), jnp.int32)

    for copy in loads:
        copy.wait()

    @pl.loop(1, specs // BLOCK)
    def _(b):
        for a in range(inputs):
            filter_block(b, a, inputs, specs, raw, taps_ref, filtered, y_high, y_low)

    @pl.when(t == 1)
    def _():
        halo.wait_recv()

    for a in range(inputs):
        filter_block(0, a, inputs, specs, raw, taps_ref, filtered, y_high, y_low)

    for copy in tables:
        copy.wait()

    @pl.loop(0, RADIX)
    def _(k1):
        for p in range(2):
            mine = slice(p * sub, (p + 1) * sub)
            mh, ml = high[k1, mine, :], low[k1, mine, :]
            yh, yl = y_high[k1], y_low[k1]
            value = lax.dot_general(mh, yh, NT, preferred_element_type=jnp.float32)
            value = value + lax.dot_general(mh, yl, NT, preferred_element_type=jnp.float32)
            value = value + lax.dot_general(ml, yh, NT, preferred_element_type=jnp.float32)
            for a in range(inputs):
                spread[pl.ds(p * inputs + a, sub, 2 * inputs), :] = value[:, a * specs : (a + 1) * specs]
        send[k1] = spread[...].astype(jnp.bfloat16).reshape(n, split * rows, specs)
        for h in range(split):
            chunk = k1 * split + h
            cut = pl.ds(h * rows, rows)
            pltpu.make_async_copy(send.at[k1, me, cut], recv.at[chunk, me], recv_sem.at[chunk]).start()

            @pl.loop(0, n - 1)
            def _(i):
                step = (i + 1) // 2
                to = lax.rem(me + n + n // 2 + step * (2 * (i % 2) - 1), n)
                pltpu.make_async_remote_copy(
                    src_ref=send.at[k1, to, cut],
                    dst_ref=recv.at[chunk, me],
                    send_sem=send_sem.at[k1],
                    recv_sem=recv_sem.at[chunk],
                    device_id={"chan": to},
                    device_id_type=pl.DeviceIdType.MESH,
                ).start()

    def exchange(chunk):
        return pltpu.make_async_remote_copy(
            src_ref=part.at[chunk, :, pl.ds(pl.multiple_of((1 - t) * half, half), half), :],
            dst_ref=other.at[chunk],
            send_sem=tm_send_sem.at[chunk],
            recv_sem=tm_recv_sem.at[chunk],
            device_id={"tm": 1 - t},
            device_id_type=pl.DeviceIdType.MESH,
        )

    def finish(chunk):
        exchange(chunk).wait_recv()
        own = part[chunk, :, pl.ds(pl.multiple_of(t * half, half), half), :]
        out_ref[chunk % split, :, chunk // split] = (own + other[chunk]) * (1.0 / (2 * specs))

    @pl.loop(0, chunks)
    def _(chunk):
        pltpu.make_async_copy(recv.at[chunk], recv.at[chunk], recv_sem.at[chunk]).wait()

        @pl.loop(0, pairs)
        def _(j):
            at = pl.multiple_of(j * 4 * inputs, 4 * inputs)
            turned = []
            for g in range(groups):
                block = recv[chunk, g * GROUP : (g + 1) * GROUP, pl.ds(at, 4 * inputs), :]
                block = block.reshape(GROUP * 4 * inputs, specs)
                turned.append(jnp.dot(perm_ref[...], block, preferred_element_type=jnp.float32).astype(jnp.bfloat16))
            run = GROUP * inputs
            for c in range(2):
                real = jnp.concatenate([x[2 * c * run : (2 * c + 1) * run] for x in turned], axis=0)
                imag = jnp.concatenate([x[(2 * c + 1) * run : (2 * c + 2) * run] for x in turned], axis=0)
                left = jnp.concatenate([real, imag], axis=1)
                right = jnp.concatenate([left, jnp.concatenate([-imag, real], axis=1)], axis=0)
                part[chunk, 2 * j + c] = lax.dot_general(left, right, NT, preferred_element_type=jnp.float32)

        exchange(chunk).start()

        @pl.when(chunk > 0)
        def _():
            finish(chunk - 1)

    finish(chunks - 1)

    @pl.when(t == 0)
    def _():
        halo.wait_send()

    @pl.loop(0, chunks)
    def _(chunk):
        exchange(chunk).wait_send()

    @pl.loop(0, RADIX)
    def _(k1):
        pltpu.make_async_copy(send.at[k1, 0 : n - 1], send.at[k1, 0 : n - 1], send_sem.at[k1]).wait()


def local_few(n, voltages):
    inputs = voltages.shape[1]
    specs = voltages.shape[2] // NCH
    tiles = NCH // LANES
    frame = tiles * inputs
    volts = voltages.reshape(2, inputs, specs * tiles, LANES).transpose(0, 2, 1, 3).reshape(2, specs * frame, LANES)
    high, low = make_dft(NCH)
    per = NCH // n // RADIX
    split = SPLIT if per % (2 * SPLIT) == 0 else 1
    chunks, each = RADIX * split, per // split
    total = n * inputs
    rows = each * 2 * inputs
    whole = pl.BlockSpec(memory_space=pltpu.VMEM)
    there = pl.BlockSpec(memory_space=pl.ANY)
    out = pl.pallas_call(
        functools.partial(kernel_few, n, inputs, specs),
        out_shape=jax.ShapeDtypeStruct((split, each, RADIX, total // 2, 2 * total), jnp.float32),
        in_specs=[there, whole, there, there, whole],
        out_specs=whole,
        scratch_shapes=[
            pltpu.VMEM((2, (specs + TAPS - 1) * frame, LANES), jnp.int32),
            pltpu.VMEM((RADIX, NCH // 2, NCH // 2), jnp.bfloat16),
            pltpu.VMEM((RADIX, NCH // 2, NCH // 2), jnp.bfloat16),
            pltpu.VMEM((2, BLOCK * tiles, LANES), jnp.float32),
            pltpu.VMEM((RADIX, inputs * specs, NCH // 2), jnp.bfloat16),
            pltpu.VMEM((RADIX, inputs * specs, NCH // 2), jnp.bfloat16),
            pltpu.VMEM((NCH // RADIX * 2 * inputs, specs), jnp.float32),
            pltpu.VMEM((RADIX, n, split * rows, specs), jnp.bfloat16),
            pltpu.VMEM((chunks, n, rows, specs), jnp.bfloat16),
            pltpu.VMEM((chunks, each, total, 2 * total), jnp.float32),
            pltpu.VMEM((chunks, each, total // 2, 2 * total), jnp.float32),
            pltpu.SemaphoreType.DMA((2,)),
            pltpu.SemaphoreType.DMA((2,)),
            pltpu.SemaphoreType.DMA,
            pltpu.SemaphoreType.DMA,
            pltpu.SemaphoreType.DMA((RADIX,)),
            pltpu.SemaphoreType.DMA((chunks,)),
            pltpu.SemaphoreType.DMA((chunks,)),
            pltpu.SemaphoreType.DMA((chunks,)),
        ],
        compiler_params=pltpu.CompilerParams(
            collective_id=0, has_side_effects=True, vmem_limit_bytes=60 * 1024 * 1024
        ),
    )(
        volts,
        jnp.asarray(make_taps(NCH).reshape(TAPS, tiles, LANES)),
        jnp.asarray(high),
        jnp.asarray(low),
        jnp.asarray(make_permutation(inputs)),
    )
    out = out.reshape(1, RADIX * per, total // 2, 2 * total)
    first = lax.broadcasted_iota(jnp.int32, (2, 1, 1, 1), 0) == 0
    return jnp.where(first, out[..., :total], out[..., total:])


def kernel(
    n,
    inputs,
    specs,
    volts_ref,
    table_ref,
    out_ref,
    raw,
    table,
    taps,
    filtered,
    y_high,
    y_low,
    send,
    recv,
    turned,
    part,
    other,
    result,
    load_sem,
    table_sem,
    halo_send_sem,
    halo_recv_sem,
    send_sem,
    recv_sem,
    tm_send_sem,
    tm_recv_sem,
    out_sem,
):
    me = lax.axis_index("chan")
    t = lax.axis_index("tm")
    sub = NCH // RADIX
    frame = NCH // LANES * inputs
    before = (TAPS - 1) * frame
    split = recv.shape[3]
    chunks = RADIX * split
    total = n * inputs
    half = total // 2

    barrier = pltpu.get_barrier_semaphore()

    @pl.loop(1, n)
    def _(i):
        pl.semaphore_signal(barrier, inc=1, device_id={"chan": lax.rem(me + i, n)}, device_id_type=pl.DeviceIdType.MESH)

    pl.semaphore_signal(barrier, inc=1, device_id={"tm": 1 - t}, device_id_type=pl.DeviceIdType.MESH)

    size = 2 * RADIX * NCH // 2
    early = pltpu.make_async_copy(table_ref.at[size:], table.at[size:], table_sem.at[0])
    late = pltpu.make_async_copy(table_ref.at[0:size], table.at[0:size], table_sem.at[1])
    early.start()
    piece = specs * frame // LOADS
    loads = [
        [
            pltpu.make_async_copy(
                volts_ref.at[p, g * piece : (g + 1) * piece, :],
                raw.at[p, before + g * piece : before + (g + 1) * piece, :],
                load_sem.at[g, p],
            )
            for p in range(2)
        ]
        for g in range(LOADS)
    ]
    for group in loads:
        for copy in group:
            copy.start()

    halo = pltpu.make_async_remote_copy(
        src_ref=volts_ref.at[:, specs * frame - before : specs * frame, :],
        dst_ref=raw.at[:, 0:before, :],
        send_sem=halo_send_sem,
        recv_sem=halo_recv_sem,
        device_id={"tm": 1 - t},
        device_id_type=pl.DeviceIdType.MESH,
    )
    pl.semaphore_wait(barrier, n)

    @pl.when(t == 0)
    def _():
        halo.start()
        raw[:, 0:before, :] = jnp.zeros((2, before, LANES), jnp.int32)

    early.wait()
    taps[...] = sum(
        table[size + i * TAPS * 8 : size + (i + 1) * TAPS * 8, 0:LANES].astype(jnp.float32) for i in range(3)
    ).reshape(TAPS, 8, LANES)

    def transform(k1, rows, length, columns):
        at = pl.multiple_of(k1 * NCH + rows, 16)
        mh, ml = table[pl.ds(at, length), :], table[pl.ds(at + NCH // 2, length), :]
        yh, yl = y_high[k1, columns, :], y_low[k1, columns, :]
        value = lax.dot_general(mh, yh, NT, preferred_element_type=jnp.float32)
        value = value + lax.dot_general(mh, yl, NT, preferred_element_type=jnp.float32)
        return value + lax.dot_general(ml, yh, NT, preferred_element_type=jnp.float32)

    mine, place = me // (n // 2), lax.rem(me, n // 2)

    def to_half(k1, cut, sem, far):
        @pl.loop(1 - far, n // 2)
        def _(i):
            side = 1 - mine if far else mine
            to = side * (n // 2) + lax.rem(place + i, n // 2)
            pltpu.make_async_remote_copy(
                src_ref=send.at[(k1, to) + cut],
                dst_ref=recv.at[(k1, me) + cut],
                send_sem=send_sem.at[k1],
                recv_sem=sem,
                device_id={"chan": to},
                device_id_type=pl.DeviceIdType.MESH,
            ).start()

    def to_partners(k1, cut, sem, order):
        for far in order:
            to_half(k1, cut, sem, far)
        pltpu.make_async_copy(send.at[(k1, me) + cut], recv.at[(k1, me) + cut], sem).start()

    for pick in [range(0, 1), range(1, 2)] + [range(a, a + 2) for a in range(2, inputs, 2)]:

        many = specs // BLOCK // LOADS
        for g in range(LOADS):
            if 0 in pick:
                for copy in loads[g]:
                    copy.wait()
                if g == LOADS - 1:
                    late.start()

            @pl.loop(max(1, g * many), (g + 1) * many)
            def _(b):
                for a in pick:
                    filter_block(b, a, inputs, specs, raw, taps, filtered, y_high, y_low)

        if 0 in pick:

            @pl.when(t == 1)
            def _():
                halo.wait_recv()

        for a in pick:
            filter_block(0, a, inputs, specs, raw, taps, filtered, y_high, y_low)
        if 0 in pick:
            late.wait()
        value = transform(0, 0, 2 * sub, slice(pick.start * specs, pick.stop * specs))
        for i, a in enumerate(pick):
            send[0, :, a] = value[:, i * specs : (i + 1) * specs].astype(jnp.bfloat16).reshape(n, split, 16, specs)
        to_partners(0, (slice(pick.start, pick.stop),), recv_sem.at[0], (1, 0))

    @pl.loop(1, RADIX)
    def _(k1):
        for p in range(2):
            value = transform(k1, p * sub, sub, slice(0, inputs * specs))
            for a in range(inputs):
                mine = value[:, a * specs : (a + 1) * specs].astype(jnp.bfloat16)
                send[k1, p * n // 2 : (p + 1) * n // 2, a] = mine.reshape(n // 2, split, 16, specs)
        for h in range(split):
            to_partners(k1, (slice(0, inputs), h), recv_sem.at[k1 * split + h], (1, 0) if h + 1 < split else (0, 1))

    def exchange(chunk, q):
        return pltpu.make_async_remote_copy(
            src_ref=part.at[chunk, 4 * q : 4 * q + 4, pl.ds(pl.multiple_of((1 - t) * half, half), half), :],
            dst_ref=other.at[chunk, 4 * q : 4 * q + 4],
            send_sem=tm_send_sem.at[chunk, q],
            recv_sem=tm_recv_sem.at[chunk, q],
            device_id={"tm": 1 - t},
            device_id_type=pl.DeviceIdType.MESH,
        )

    def store(chunk, q):
        return pltpu.make_async_copy(
            result.at[chunk, :, 4 * q : 4 * q + 4],
            out_ref.at[:, chunk % split, 4 * q : 4 * q + 4, chunk // split],
            out_sem.at[chunk, q],
        )

    def finish(chunk):
        for q in range(2):
            exchange(chunk, q).wait_recv()
            own = part[chunk, 4 * q : 4 * q + 4, pl.ds(pl.multiple_of(t * half, half), half), :]
            value = (own + other[chunk, 4 * q : 4 * q + 4]) * (1.0 / (2 * specs))
            result[chunk, 0, 4 * q : 4 * q + 4] = value[:, :, :total]
            result[chunk, 1, 4 * q : 4 * q + 4] = value[:, :, total:]
            store(chunk, q).start()

    @pl.loop(0, chunks)
    def _(chunk):
        k1, h = chunk // split, chunk % split

        @pl.when(chunk == 0)
        def _():
            pltpu.make_async_copy(recv.at[0], recv.at[0], recv_sem.at[0]).wait()

        @pl.when(chunk >= split)
        def _():
            came = recv.at[k1, :, :, h]
            pltpu.make_async_copy(came, came, recv_sem.at[chunk]).wait()

        turned[...] = recv[k1, :, :, h].astype(jnp.float32).reshape(total * 16, specs)
        for c in range(8):
            real = turned[pl.ds(c, total, 16), :].astype(jnp.bfloat16)
            imag = turned[pl.ds(8 + c, total, 16), :].astype(jnp.bfloat16)
            left = jnp.concatenate([real, imag], axis=1)
            right = jnp.concatenate([left, jnp.concatenate([-imag, real], axis=1)], axis=0)
            part[chunk, c] = lax.dot_general(left, right, NT, preferred_element_type=jnp.float32)
            if c % 4 == 3:
                exchange(chunk, c // 4).start()

        @pl.when(chunk > 0)
        def _():
            finish(chunk - 1)

    finish(chunks - 1)

    @pl.when(t == 0)
    def _():
        halo.wait_send()

    @pl.loop(0, chunks)
    def _(chunk):
        for q in range(2):
            exchange(chunk, q).wait_send()
            store(chunk, q).wait()

    @pl.loop(0, RADIX)
    def _(k1):
        pltpu.make_async_copy(send.at[k1, 0 : n - 1], send.at[k1, 0 : n - 1], send_sem.at[k1]).wait()


def local(n, voltages):
    inputs = voltages.shape[1]
    specs = voltages.shape[2] // NCH
    per = NCH // n // RADIX
    if per % 8:
        return local_few(n, voltages)
    tiles = NCH // LANES
    frame = tiles * inputs
    volts = voltages.reshape(2, inputs, specs * tiles, LANES).transpose(0, 2, 1, 3).reshape(2, specs * frame, LANES)
    high, low = make_dft(NCH)
    parts, rest = [], make_taps(NCH).reshape(-1, LANES)
    for _ in range(3):
        parts.append(rest.astype(ml_dtypes.bfloat16))
        rest = rest - parts[-1].astype(np.float32)
    parts = np.pad(np.concatenate(parts), ((0, 0), (0, NCH // 2 - LANES)))
    split = per // 8
    chunks = RADIX * split
    total = n * inputs

    def tiled(m):
        return m.reshape(RADIX, 2, NCH // RADIX // 8, 8, NCH // 2).transpose(0, 2, 1, 3, 4).reshape(m.shape)

    table = np.stack([tiled(high), tiled(low)], axis=1).reshape(-1, NCH // 2)
    table = np.concatenate([table, parts])
    there = pl.BlockSpec(memory_space=pltpu.HBM)
    out = pl.pallas_call(
        functools.partial(kernel, n, inputs, specs),
        out_shape=jax.ShapeDtypeStruct((2, split, 8, RADIX, total // 2, total), jnp.float32),
        in_specs=[there, there],
        out_specs=pl.BlockSpec(memory_space=pl.ANY),
        scratch_shapes=[
            pltpu.VMEM((2, (specs + TAPS - 1) * frame, LANES), jnp.int32),
            pltpu.VMEM(table.shape, jnp.bfloat16),
            pltpu.VMEM((TAPS, tiles, LANES), jnp.float32),
            pltpu.VMEM((2, BLOCK * tiles, LANES), jnp.float32),
            pltpu.VMEM((RADIX, inputs * specs, NCH // 2), jnp.bfloat16),
            pltpu.VMEM((RADIX, inputs * specs, NCH // 2), jnp.bfloat16),
            pltpu.VMEM((RADIX, n, inputs, split, 16, specs), jnp.bfloat16),
            pltpu.VMEM((RADIX, n, inputs, split, 16, specs), jnp.bfloat16),
            pltpu.VMEM((total * 16, specs), jnp.float32),
            pltpu.VMEM((chunks, 8, total, 2 * total), jnp.float32),
            pltpu.VMEM((chunks, 8, total // 2, 2 * total), jnp.float32),
            pltpu.VMEM((chunks, 2, 8, total // 2, total), jnp.float32),
            pltpu.SemaphoreType.DMA((LOADS, 2)),
            pltpu.SemaphoreType.DMA((2,)),
            pltpu.SemaphoreType.DMA,
            pltpu.SemaphoreType.DMA,
            pltpu.SemaphoreType.DMA((RADIX,)),
            pltpu.SemaphoreType.DMA((chunks,)),
            pltpu.SemaphoreType.DMA((chunks, 2)),
            pltpu.SemaphoreType.DMA((chunks, 2)),
            pltpu.SemaphoreType.DMA((chunks, 2)),
        ],
        compiler_params=pltpu.CompilerParams(
            collective_id=0, has_side_effects=True, vmem_limit_bytes=VMEM * 1024 * 1024
        ),
    )(volts, jnp.asarray(table))
    return out.reshape(2, RADIX * per, total // 2, total)


def solution(mesh):
    placed = (P(None, "chan", "tm"),)
    return jax.shard_map(
        functools.partial(local, mesh.shape["chan"]),
        mesh=mesh,
        in_specs=placed,
        out_specs=P(None, "chan", "tm", None),
        check_vma=False,
    )
```

```python
import functools

import jax
import jax.numpy as jnp
import ml_dtypes
import numpy as np
from jax import lax
from jax.experimental import pallas as pl
from jax.experimental.pallas import tpu as pltpu
from jax.sharding import PartitionSpec as P

NCH = 1024
TAPS = 4
RADIX = 4
GROUP = 16
LANES = 128
BLOCK = 16
SPLIT = 2
LOADS = 4
VMEM = 50
NT = (((1,), (1,)), ((), ()))


def make_taps(nch):
    k = np.arange(TAPS * nch, dtype=np.float64)
    x = (k - 2.0 * nch + 0.5) / nch
    window = 0.54 - 0.46 * np.cos(2.0 * np.pi * (k + 0.5) / (TAPS * nch))
    return (np.sinc(x) * window).reshape(TAPS, nch).astype(np.float32)


def make_dft(nch):
    sub = nch // RADIX
    n = np.arange(sub)
    highs, lows = [], []
    for r in range(RADIX):
        k = RADIX * np.arange(sub) + r
        angle = (k[:, None] * n[None, :] % nch) * (2.0 * np.pi / nch)
        c, s = np.cos(angle), np.sin(angle)
        m = np.block([[c, s], [-s, c]]) * (0.25 / np.sqrt(nch))
        high = m.astype(np.float32).astype(ml_dtypes.bfloat16)
        low = (m - high.astype(np.float64)).astype(np.float32).astype(ml_dtypes.bfloat16)
        highs.append(high)
        lows.append(low)
    return np.stack(highs), np.stack(lows)


def make_permutation(local_inputs):
    size = GROUP * 4 * local_inputs
    order = np.arange(size).reshape(GROUP, 2, 2, local_inputs).transpose(1, 2, 0, 3).reshape(-1)
    perm = np.zeros((size, size), np.float32)
    perm[np.arange(size), order] = 1.0
    return perm.astype(ml_dtypes.bfloat16)


def filter_block(b, a, inputs, specs, raw, taps_ref, filtered, y_high, y_low):
    sub = NCH // RADIX
    tiles = NCH // LANES
    frame = tiles * inputs
    at = b * BLOCK
    for p in range(2):
        frames = raw[p, pl.ds(at * frame + a, (BLOCK + TAPS - 1) * tiles, inputs), :].astype(jnp.float32)
        frames = frames.reshape(BLOCK + TAPS - 1, tiles, LANES)
        value = taps_ref[0] * frames[0:BLOCK]
        for step in range(1, TAPS):
            value = value + taps_ref[step] * frames[step : step + BLOCK]
        filtered[p] = value.reshape(BLOCK * tiles, LANES)
    quarter = tiles // RADIX
    place = pl.ds(pl.multiple_of(a * specs + at, BLOCK), BLOCK)
    for h in range(quarter):
        r, im = [[filtered[p, pl.ds(q * quarter + h, BLOCK, tiles), :] for q in range(RADIX)] for p in range(2)]
        er, orr, dr, gr = r[0] + r[2], r[1] + r[3], r[0] - r[2], r[1] - r[3]
        ei, oi, di, gi = im[0] + im[2], im[1] + im[3], im[0] - im[2], im[1] - im[3]
        parts = [(er + orr, ei + oi), (dr + gi, di - gr), (er - orr, ei - oi), (dr - gi, di + gr)]
        for k1 in range(RADIX):
            for p in range(2):
                value = parts[k1][p]
                top = value.astype(jnp.bfloat16)
                lanes = slice(p * sub + h * LANES, p * sub + (h + 1) * LANES)
                y_high[k1, place, lanes] = top
                y_low[k1, place, lanes] = (value - top.astype(jnp.float32)).astype(jnp.bfloat16)


def kernel_few(
    n,
    inputs,
    specs,
    volts_ref,
    taps_ref,
    high_ref,
    low_ref,
    perm_ref,
    out_ref,
    raw,
    high,
    low,
    filtered,
    y_high,
    y_low,
    spread,
    send,
    recv,
    part,
    other,
    load_sem,
    table_sem,
    halo_send_sem,
    halo_recv_sem,
    send_sem,
    recv_sem,
    tm_send_sem,
    tm_recv_sem,
):
    me = lax.axis_index("chan")
    t = lax.axis_index("tm")
    sub = NCH // RADIX
    tiles = NCH // LANES
    frame = tiles * inputs
    before = (TAPS - 1) * frame
    chunks = recv.shape[0]
    split = chunks // RADIX
    rows = recv.shape[2]
    pairs = rows // (4 * inputs)
    groups = n // GROUP
    half = n * inputs // 2

    barrier = pltpu.get_barrier_semaphore()

    @pl.loop(1, n)
    def _(i):
        pl.semaphore_signal(barrier, inc=1, device_id={"chan": lax.rem(me + i, n)}, device_id_type=pl.DeviceIdType.MESH)

    pl.semaphore_signal(barrier, inc=1, device_id={"tm": 1 - t}, device_id_type=pl.DeviceIdType.MESH)

    loads = [
        pltpu.make_async_copy(volts_ref.at[p], raw.at[p, before : before + specs * frame, :], load_sem.at[p])
        for p in range(2)
    ]
    tables = [
        pltpu.make_async_copy(high_ref, high, table_sem.at[0]),
        pltpu.make_async_copy(low_ref, low, table_sem.at[1]),
    ]
    for copy in loads + tables:
        copy.start()

    halo = pltpu.make_async_remote_copy(
        src_ref=volts_ref.at[:, specs * frame - before : specs * frame, :],
        dst_ref=raw.at[:, 0:before, :],
        send_sem=halo_send_sem,
        recv_sem=halo_recv_sem,
        device_id={"tm": 1 - t},
        device_id_type=pl.DeviceIdType.MESH,
    )
    pl.semaphore_wait(barrier, n)

    @pl.when(t == 0)
    def _():
        halo.start()
        raw[:, 0:before, :] = jnp.zeros((2, before, LANES), jnp.int32)

    for copy in loads:
        copy.wait()

    @pl.loop(1, specs // BLOCK)
    def _(b):
        for a in range(inputs):
            filter_block(b, a, inputs, specs, raw, taps_ref, filtered, y_high, y_low)

    @pl.when(t == 1)
    def _():
        halo.wait_recv()

    for a in range(inputs):
        filter_block(0, a, inputs, specs, raw, taps_ref, filtered, y_high, y_low)

    for copy in tables:
        copy.wait()

    @pl.loop(0, RADIX)
    def _(k1):
        for p in range(2):
            mine = slice(p * sub, (p + 1) * sub)
            mh, ml = high[k1, mine, :], low[k1, mine, :]
            yh, yl = y_high[k1], y_low[k1]
            value = lax.dot_general(mh, yh, NT, preferred_element_type=jnp.float32)
            value = value + lax.dot_general(mh, yl, NT, preferred_element_type=jnp.float32)
            value = value + lax.dot_general(ml, yh, NT, preferred_element_type=jnp.float32)
            for a in range(inputs):
                spread[pl.ds(p * inputs + a, sub, 2 * inputs), :] = value[:, a * specs : (a + 1) * specs]
        send[k1] = spread[...].astype(jnp.bfloat16).reshape(n, split * rows, specs)
        for h in range(split):
            chunk = k1 * split + h
            cut = pl.ds(h * rows, rows)
            pltpu.make_async_copy(send.at[k1, me, cut], recv.at[chunk, me], recv_sem.at[chunk]).start()

            @pl.loop(0, n - 1)
            def _(i):
                step = (i + 1) // 2
                to = lax.rem(me + n + n // 2 + step * (2 * (i % 2) - 1), n)
                pltpu.make_async_remote_copy(
                    src_ref=send.at[k1, to, cut],
                    dst_ref=recv.at[chunk, me],
                    send_sem=send_sem.at[k1],
                    recv_sem=recv_sem.at[chunk],
                    device_id={"chan": to},
                    device_id_type=pl.DeviceIdType.MESH,
                ).start()

    def exchange(chunk):
        return pltpu.make_async_remote_copy(
            src_ref=part.at[chunk, :, pl.ds(pl.multiple_of((1 - t) * half, half), half), :],
            dst_ref=other.at[chunk],
            send_sem=tm_send_sem.at[chunk],
            recv_sem=tm_recv_sem.at[chunk],
            device_id={"tm": 1 - t},
            device_id_type=pl.DeviceIdType.MESH,
        )

    def finish(chunk):
        exchange(chunk).wait_recv()
        own = part[chunk, :, pl.ds(pl.multiple_of(t * half, half), half), :]
        out_ref[chunk % split, :, chunk // split] = (own + other[chunk]) * (1.0 / (2 * specs))

    @pl.loop(0, chunks)
    def _(chunk):
        pltpu.make_async_copy(recv.at[chunk], recv.at[chunk], recv_sem.at[chunk]).wait()

        @pl.loop(0, pairs)
        def _(j):
            at = pl.multiple_of(j * 4 * inputs, 4 * inputs)
            turned = []
            for g in range(groups):
                block = recv[chunk, g * GROUP : (g + 1) * GROUP, pl.ds(at, 4 * inputs), :]
                block = block.reshape(GROUP * 4 * inputs, specs)
                turned.append(jnp.dot(perm_ref[...], block, preferred_element_type=jnp.float32).astype(jnp.bfloat16))
            run = GROUP * inputs
            for c in range(2):
                real = jnp.concatenate([x[2 * c * run : (2 * c + 1) * run] for x in turned], axis=0)
                imag = jnp.concatenate([x[(2 * c + 1) * run : (2 * c + 2) * run] for x in turned], axis=0)
                left = jnp.concatenate([real, imag], axis=1)
                right = jnp.concatenate([left, jnp.concatenate([-imag, real], axis=1)], axis=0)
                part[chunk, 2 * j + c] = lax.dot_general(left, right, NT, preferred_element_type=jnp.float32)

        exchange(chunk).start()

        @pl.when(chunk > 0)
        def _():
            finish(chunk - 1)

    finish(chunks - 1)

    @pl.when(t == 0)
    def _():
        halo.wait_send()

    @pl.loop(0, chunks)
    def _(chunk):
        exchange(chunk).wait_send()

    @pl.loop(0, RADIX)
    def _(k1):
        pltpu.make_async_copy(send.at[k1, 0 : n - 1], send.at[k1, 0 : n - 1], send_sem.at[k1]).wait()


def local_few(n, voltages):
    inputs = voltages.shape[1]
    specs = voltages.shape[2] // NCH
    tiles = NCH // LANES
    frame = tiles * inputs
    volts = voltages.reshape(2, inputs, specs * tiles, LANES).transpose(0, 2, 1, 3).reshape(2, specs * frame, LANES)
    high, low = make_dft(NCH)
    per = NCH // n // RADIX
    split = SPLIT if per % (2 * SPLIT) == 0 else 1
    chunks, each = RADIX * split, per // split
    total = n * inputs
    rows = each * 2 * inputs
    whole = pl.BlockSpec(memory_space=pltpu.VMEM)
    there = pl.BlockSpec(memory_space=pl.ANY)
    out = pl.pallas_call(
        functools.partial(kernel_few, n, inputs, specs),
        out_shape=jax.ShapeDtypeStruct((split, each, RADIX, total // 2, 2 * total), jnp.float32),
        in_specs=[there, whole, there, there, whole],
        out_specs=whole,
        scratch_shapes=[
            pltpu.VMEM((2, (specs + TAPS - 1) * frame, LANES), jnp.int32),
            pltpu.VMEM((RADIX, NCH // 2, NCH // 2), jnp.bfloat16),
            pltpu.VMEM((RADIX, NCH // 2, NCH // 2), jnp.bfloat16),
            pltpu.VMEM((2, BLOCK * tiles, LANES), jnp.float32),
            pltpu.VMEM((RADIX, inputs * specs, NCH // 2), jnp.bfloat16),
            pltpu.VMEM((RADIX, inputs * specs, NCH // 2), jnp.bfloat16),
            pltpu.VMEM((NCH // RADIX * 2 * inputs, specs), jnp.float32),
            pltpu.VMEM((RADIX, n, split * rows, specs), jnp.bfloat16),
            pltpu.VMEM((chunks, n, rows, specs), jnp.bfloat16),
            pltpu.VMEM((chunks, each, total, 2 * total), jnp.float32),
            pltpu.VMEM((chunks, each, total // 2, 2 * total), jnp.float32),
            pltpu.SemaphoreType.DMA((2,)),
            pltpu.SemaphoreType.DMA((2,)),
            pltpu.SemaphoreType.DMA,
            pltpu.SemaphoreType.DMA,
            pltpu.SemaphoreType.DMA((RADIX,)),
            pltpu.SemaphoreType.DMA((chunks,)),
            pltpu.SemaphoreType.DMA((chunks,)),
            pltpu.SemaphoreType.DMA((chunks,)),
        ],
        compiler_params=pltpu.CompilerParams(
            collective_id=0, has_side_effects=True, vmem_limit_bytes=60 * 1024 * 1024
        ),
    )(
        volts,
        jnp.asarray(make_taps(NCH).reshape(TAPS, tiles, LANES)),
        jnp.asarray(high),
        jnp.asarray(low),
        jnp.asarray(make_permutation(inputs)),
    )
    out = out.reshape(1, RADIX * per, total // 2, 2 * total)
    first = lax.broadcasted_iota(jnp.int32, (2, 1, 1, 1), 0) == 0
    return jnp.where(first, out[..., :total], out[..., total:])


def kernel(
    n,
    inputs,
    specs,
    volts_ref,
    table_ref,
    out_ref,
    raw,
    table,
    taps,
    filtered,
    y_high,
    y_low,
    send,
    recv,
    turned,
    part,
    other,
    result,
    load_sem,
    table_sem,
    halo_send_sem,
    halo_recv_sem,
    send_sem,
    recv_sem,
    tm_send_sem,
    tm_recv_sem,
    out_sem,
):
    me = lax.axis_index("chan")
    t = lax.axis_index("tm")
    sub = NCH // RADIX
    frame = NCH // LANES * inputs
    before = (TAPS - 1) * frame
    split = recv.shape[2]
    chunks = RADIX * split
    total = n * inputs
    half = total // 2

    barrier = pltpu.get_barrier_semaphore()

    @pl.loop(1, n)
    def _(i):
        pl.semaphore_signal(barrier, inc=1, device_id={"chan": lax.rem(me + i, n)}, device_id_type=pl.DeviceIdType.MESH)

    pl.semaphore_signal(barrier, inc=1, device_id={"tm": 1 - t}, device_id_type=pl.DeviceIdType.MESH)

    size = 2 * RADIX * NCH // 2
    early = pltpu.make_async_copy(table_ref.at[size:], table.at[size:], table_sem.at[0])
    late = pltpu.make_async_copy(table_ref.at[0:size], table.at[0:size], table_sem.at[1])
    early.start()
    piece = specs * frame // LOADS
    loads = [
        [
            pltpu.make_async_copy(
                volts_ref.at[p, g * piece : (g + 1) * piece, :],
                raw.at[p, before + g * piece : before + (g + 1) * piece, :],
                load_sem.at[g, p],
            )
            for p in range(2)
        ]
        for g in range(LOADS)
    ]
    for group in loads:
        for copy in group:
            copy.start()

    halo = pltpu.make_async_remote_copy(
        src_ref=volts_ref.at[:, specs * frame - before : specs * frame, :],
        dst_ref=raw.at[:, 0:before, :],
        send_sem=halo_send_sem,
        recv_sem=halo_recv_sem,
        device_id={"tm": 1 - t},
        device_id_type=pl.DeviceIdType.MESH,
    )
    pl.semaphore_wait(barrier, n)

    @pl.when(t == 0)
    def _():
        halo.start()
        raw[:, 0:before, :] = jnp.zeros((2, before, LANES), jnp.int32)

    early.wait()
    taps[...] = sum(
        table[size + i * TAPS * 8 : size + (i + 1) * TAPS * 8, 0:LANES].astype(jnp.float32) for i in range(3)
    ).reshape(TAPS, 8, LANES)

    def transform(k1, rows, length, columns):
        at = pl.multiple_of(k1 * NCH + rows, 16)
        mh, ml = table[pl.ds(at, length), :], table[pl.ds(at + NCH // 2, length), :]
        yh, yl = y_high[k1, columns, :], y_low[k1, columns, :]
        value = lax.dot_general(mh, yh, NT, preferred_element_type=jnp.float32)
        value = value + lax.dot_general(mh, yl, NT, preferred_element_type=jnp.float32)
        return value + lax.dot_general(ml, yh, NT, preferred_element_type=jnp.float32)

    mine, place = me // (n // 2), lax.rem(me, n // 2)

    def to_half(k1, cut, sem, far):
        @pl.loop(1 - far, n // 2)
        def _(i):
            side = 1 - mine if far else mine
            to = side * (n // 2) + lax.rem(place + i, n // 2)
            pltpu.make_async_remote_copy(
                src_ref=send.at[(k1, to) + cut],
                dst_ref=recv.at[(k1, me) + cut],
                send_sem=send_sem.at[k1],
                recv_sem=sem,
                device_id={"chan": to},
                device_id_type=pl.DeviceIdType.MESH,
            ).start()

    def to_partners(k1, cut, sem, order):
        for far in order:
            to_half(k1, cut, sem, far)
        pltpu.make_async_copy(send.at[(k1, me) + cut], recv.at[(k1, me) + cut], sem).start()

    for pick in [range(0, 1), range(1, 2)] + [range(a, a + 2) for a in range(2, inputs, 2)]:

        many = specs // BLOCK // LOADS
        for g in range(LOADS):
            if 0 in pick:
                for copy in loads[g]:
                    copy.wait()
                if g == LOADS - 1:
                    late.start()

            @pl.loop(max(1, g * many), (g + 1) * many)
            def _(b):
                for a in pick:
                    filter_block(b, a, inputs, specs, raw, taps, filtered, y_high, y_low)

        if 0 in pick:

            @pl.when(t == 1)
            def _():
                halo.wait_recv()

        for a in pick:
            filter_block(0, a, inputs, specs, raw, taps, filtered, y_high, y_low)
        if 0 in pick:
            late.wait()
        value = transform(0, 0, 2 * sub, slice(pick.start * specs, pick.stop * specs))
        for i, a in enumerate(pick):
            send[0, :, :, a] = value[:, i * specs : (i + 1) * specs].astype(jnp.bfloat16).reshape(n, split, 16, specs)
        to_partners(0, (slice(0, split), slice(pick.start, pick.stop)), recv_sem.at[0], (1, 0))

    def issue(k1):
        for p in range(2):
            value = transform(k1, p * sub, sub, slice(0, inputs * specs))
            for a in range(inputs):
                mine = value[:, a * specs : (a + 1) * specs].astype(jnp.bfloat16)
                send[k1, p * n // 2 : (p + 1) * n // 2, :, a] = mine.reshape(n // 2, split, 16, specs)
        for h in range(split):
            to_partners(k1, (h,), recv_sem.at[k1 * split + h], (1, 0) if h + 1 < split else (0, 1))

    def sent(k1):
        left = send.at[k1, 0 : n - 1]
        return pltpu.make_async_copy(left, left, send_sem.at[k1])

    def exchange(chunk, q):
        return pltpu.make_async_remote_copy(
            src_ref=part.at[chunk, 4 * q : 4 * q + 4, pl.ds(pl.multiple_of((1 - t) * half, half), half), :],
            dst_ref=other.at[chunk, 4 * q : 4 * q + 4],
            send_sem=tm_send_sem.at[chunk, q],
            recv_sem=tm_recv_sem.at[chunk, q],
            device_id={"tm": 1 - t},
            device_id_type=pl.DeviceIdType.MESH,
        )

    def store(chunk, q):
        return pltpu.make_async_copy(
            result.at[chunk, :, 4 * q : 4 * q + 4],
            out_ref.at[:, chunk % split, 4 * q : 4 * q + 4, chunk // split],
            out_sem.at[chunk, q],
        )

    def finish(chunk):
        for q in range(2):
            exchange(chunk, q).wait_recv()
            own = part[chunk, 4 * q : 4 * q + 4, pl.ds(pl.multiple_of(t * half, half), half), :]
            value = (own + other[chunk, 4 * q : 4 * q + 4]) * (1.0 / (2 * specs))
            result[chunk, 0, 4 * q : 4 * q + 4] = value[:, :, :total]
            result[chunk, 1, 4 * q : 4 * q + 4] = value[:, :, total:]
            store(chunk, q).start()

    issue(1)

    @pl.loop(0, chunks)
    def _(chunk):
        k1, h = chunk // split, chunk % split

        @pl.when((h == 0) & (k1 + 2 < RADIX))
        def _():
            sent(k1).wait()
            issue(k1 + 2)

        @pl.when(chunk == 0)
        def _():
            pltpu.make_async_copy(recv.at[0], recv.at[0], recv_sem.at[0]).wait()

        @pl.when(chunk >= split)
        def _():
            came = recv.at[k1, :, h]
            pltpu.make_async_copy(came, came, recv_sem.at[chunk]).wait()

        turned[...] = recv[k1, :, h].astype(jnp.float32).reshape(total * 16, specs)
        for c in range(8):
            real = turned[pl.ds(c, total, 16), :].astype(jnp.bfloat16)
            imag = turned[pl.ds(8 + c, total, 16), :].astype(jnp.bfloat16)
            left = jnp.concatenate([real, imag], axis=1)
            right = jnp.concatenate([left, jnp.concatenate([-imag, real], axis=1)], axis=0)
            part[chunk, c] = lax.dot_general(left, right, NT, preferred_element_type=jnp.float32)
            if c % 4 == 3:
                exchange(chunk, c // 4).start()

        @pl.when(chunk > 0)
        def _():
            finish(chunk - 1)

    finish(chunks - 1)

    @pl.when(t == 0)
    def _():
        halo.wait_send()

    @pl.loop(0, chunks)
    def _(chunk):
        for q in range(2):
            exchange(chunk, q).wait_send()
            store(chunk, q).wait()

    for k1 in range(RADIX - 2, RADIX):
        sent(k1).wait()


def local(n, voltages):
    inputs = voltages.shape[1]
    specs = voltages.shape[2] // NCH
    per = NCH // n // RADIX
    if per % 8:
        return local_few(n, voltages)
    tiles = NCH // LANES
    frame = tiles * inputs
    volts = voltages.reshape(2, inputs, specs * tiles, LANES).transpose(0, 2, 1, 3).reshape(2, specs * frame, LANES)
    high, low = make_dft(NCH)
    parts, rest = [], make_taps(NCH).reshape(-1, LANES)
    for _ in range(3):
        parts.append(rest.astype(ml_dtypes.bfloat16))
        rest = rest - parts[-1].astype(np.float32)
    parts = np.pad(np.concatenate(parts), ((0, 0), (0, NCH // 2 - LANES)))
    split = per // 8
    chunks = RADIX * split
    total = n * inputs

    def tiled(m):
        return m.reshape(RADIX, 2, NCH // RADIX // 8, 8, NCH // 2).transpose(0, 2, 1, 3, 4).reshape(m.shape)

    table = np.stack([tiled(high), tiled(low)], axis=1).reshape(-1, NCH // 2)
    table = np.concatenate([table, parts])
    there = pl.BlockSpec(memory_space=pltpu.HBM)
    out = pl.pallas_call(
        functools.partial(kernel, n, inputs, specs),
        out_shape=jax.ShapeDtypeStruct((2, split, 8, RADIX, total // 2, total), jnp.float32),
        in_specs=[there, there],
        out_specs=pl.BlockSpec(memory_space=pl.ANY),
        scratch_shapes=[
            pltpu.VMEM((2, (specs + TAPS - 1) * frame, LANES), jnp.int32),
            pltpu.VMEM(table.shape, jnp.bfloat16),
            pltpu.VMEM((TAPS, tiles, LANES), jnp.float32),
            pltpu.VMEM((2, BLOCK * tiles, LANES), jnp.float32),
            pltpu.VMEM((RADIX, inputs * specs, NCH // 2), jnp.bfloat16),
            pltpu.VMEM((RADIX, inputs * specs, NCH // 2), jnp.bfloat16),
            pltpu.VMEM((RADIX, n, split, inputs, 16, specs), jnp.bfloat16),
            pltpu.VMEM((RADIX, n, split, inputs, 16, specs), jnp.bfloat16),
            pltpu.VMEM((total * 16, specs), jnp.float32),
            pltpu.VMEM((chunks, 8, total, 2 * total), jnp.float32),
            pltpu.VMEM((chunks, 8, total // 2, 2 * total), jnp.float32),
            pltpu.VMEM((chunks, 2, 8, total // 2, total), jnp.float32),
            pltpu.SemaphoreType.DMA((LOADS, 2)),
            pltpu.SemaphoreType.DMA((2,)),
            pltpu.SemaphoreType.DMA,
            pltpu.SemaphoreType.DMA,
            pltpu.SemaphoreType.DMA((RADIX,)),
            pltpu.SemaphoreType.DMA((chunks,)),
            pltpu.SemaphoreType.DMA((chunks, 2)),
            pltpu.SemaphoreType.DMA((chunks, 2)),
            pltpu.SemaphoreType.DMA((chunks, 2)),
        ],
        compiler_params=pltpu.CompilerParams(
            collective_id=0, has_side_effects=True, vmem_limit_bytes=VMEM * 1024 * 1024
        ),
    )(volts, jnp.asarray(table))
    return out.reshape(2, RADIX * per, total // 2, total)


def solution(mesh):
    placed = (P(None, "chan", "tm"),)
    return jax.shard_map(
        functools.partial(local, mesh.shape["chan"]),
        mesh=mesh,
        in_specs=placed,
        out_specs=P(None, "chan", "tm", None),
        check_vma=False,
    )
```

```python
import functools

import jax
import jax.numpy as jnp
import ml_dtypes
import numpy as np
from jax import lax
from jax.experimental import pallas as pl
from jax.experimental.pallas import tpu as pltpu
from jax.sharding import PartitionSpec as P

NCH = 1024
TAPS = 4
RADIX = 4
GROUP = 16
LANES = 128
BLOCK = 16
SPLIT = 2
LOADS = 4
VMEM = 50
NT = (((1,), (1,)), ((), ()))


def make_taps(nch):
    k = np.arange(TAPS * nch, dtype=np.float64)
    x = (k - 2.0 * nch + 0.5) / nch
    window = 0.54 - 0.46 * np.cos(2.0 * np.pi * (k + 0.5) / (TAPS * nch))
    return (np.sinc(x) * window).reshape(TAPS, nch).astype(np.float32)


def make_dft(nch):
    sub = nch // RADIX
    n = np.arange(sub)
    highs, lows = [], []
    for r in range(RADIX):
        k = RADIX * np.arange(sub) + r
        angle = (k[:, None] * n[None, :] % nch) * (2.0 * np.pi / nch)
        c, s = np.cos(angle), np.sin(angle)
        m = np.block([[c, s], [-s, c]]) * (0.25 / np.sqrt(nch))
        high = m.astype(np.float32).astype(ml_dtypes.bfloat16)
        low = (m - high.astype(np.float64)).astype(np.float32).astype(ml_dtypes.bfloat16)
        highs.append(high)
        lows.append(low)
    return np.stack(highs), np.stack(lows)


def make_permutation(local_inputs):
    size = GROUP * 4 * local_inputs
    order = np.arange(size).reshape(GROUP, 2, 2, local_inputs).transpose(1, 2, 0, 3).reshape(-1)
    perm = np.zeros((size, size), np.float32)
    perm[np.arange(size), order] = 1.0
    return perm.astype(ml_dtypes.bfloat16)


def filter_block(b, a, inputs, specs, raw, taps_ref, filtered, y_high, y_low):
    sub = NCH // RADIX
    tiles = NCH // LANES
    frame = tiles * inputs
    at = b * BLOCK
    for p in range(2):
        frames = raw[p, pl.ds(at * frame + a, (BLOCK + TAPS - 1) * tiles, inputs), :].astype(jnp.float32)
        frames = frames.reshape(BLOCK + TAPS - 1, tiles, LANES)
        value = taps_ref[0] * frames[0:BLOCK]
        for step in range(1, TAPS):
            value = value + taps_ref[step] * frames[step : step + BLOCK]
        filtered[p] = value.reshape(BLOCK * tiles, LANES)
    quarter = tiles // RADIX
    place = pl.ds(pl.multiple_of(a * specs + at, BLOCK), BLOCK)
    for h in range(quarter):
        r, im = [[filtered[p, pl.ds(q * quarter + h, BLOCK, tiles), :] for q in range(RADIX)] for p in range(2)]
        er, orr, dr, gr = r[0] + r[2], r[1] + r[3], r[0] - r[2], r[1] - r[3]
        ei, oi, di, gi = im[0] + im[2], im[1] + im[3], im[0] - im[2], im[1] - im[3]
        parts = [(er + orr, ei + oi), (dr + gi, di - gr), (er - orr, ei - oi), (dr - gi, di + gr)]
        for k1 in range(RADIX):
            for p in range(2):
                value = parts[k1][p]
                top = value.astype(jnp.bfloat16)
                lanes = slice(p * sub + h * LANES, p * sub + (h + 1) * LANES)
                y_high[k1, place, lanes] = top
                y_low[k1, place, lanes] = (value - top.astype(jnp.float32)).astype(jnp.bfloat16)


def kernel_few(
    n,
    inputs,
    specs,
    volts_ref,
    taps_ref,
    high_ref,
    low_ref,
    perm_ref,
    out_ref,
    raw,
    high,
    low,
    filtered,
    y_high,
    y_low,
    spread,
    send,
    recv,
    part,
    other,
    load_sem,
    table_sem,
    halo_send_sem,
    halo_recv_sem,
    send_sem,
    recv_sem,
    tm_send_sem,
    tm_recv_sem,
):
    me = lax.axis_index("chan")
    t = lax.axis_index("tm")
    sub = NCH // RADIX
    tiles = NCH // LANES
    frame = tiles * inputs
    before = (TAPS - 1) * frame
    chunks = recv.shape[0]
    split = chunks // RADIX
    rows = recv.shape[2]
    pairs = rows // (4 * inputs)
    groups = n // GROUP
    half = n * inputs // 2

    barrier = pltpu.get_barrier_semaphore()

    @pl.loop(1, n)
    def _(i):
        pl.semaphore_signal(barrier, inc=1, device_id={"chan": lax.rem(me + i, n)}, device_id_type=pl.DeviceIdType.MESH)

    pl.semaphore_signal(barrier, inc=1, device_id={"tm": 1 - t}, device_id_type=pl.DeviceIdType.MESH)

    loads = [
        pltpu.make_async_copy(volts_ref.at[p], raw.at[p, before : before + specs * frame, :], load_sem.at[p])
        for p in range(2)
    ]
    tables = [
        pltpu.make_async_copy(high_ref, high, table_sem.at[0]),
        pltpu.make_async_copy(low_ref, low, table_sem.at[1]),
    ]
    for copy in loads + tables:
        copy.start()

    halo = pltpu.make_async_remote_copy(
        src_ref=volts_ref.at[:, specs * frame - before : specs * frame, :],
        dst_ref=raw.at[:, 0:before, :],
        send_sem=halo_send_sem,
        recv_sem=halo_recv_sem,
        device_id={"tm": 1 - t},
        device_id_type=pl.DeviceIdType.MESH,
    )
    pl.semaphore_wait(barrier, n)

    @pl.when(t == 0)
    def _():
        halo.start()
        raw[:, 0:before, :] = jnp.zeros((2, before, LANES), jnp.int32)

    for copy in loads:
        copy.wait()

    @pl.loop(1, specs // BLOCK)
    def _(b):
        for a in range(inputs):
            filter_block(b, a, inputs, specs, raw, taps_ref, filtered, y_high, y_low)

    @pl.when(t == 1)
    def _():
        halo.wait_recv()

    for a in range(inputs):
        filter_block(0, a, inputs, specs, raw, taps_ref, filtered, y_high, y_low)

    for copy in tables:
        copy.wait()

    @pl.loop(0, RADIX)
    def _(k1):
        for p in range(2):
            mine = slice(p * sub, (p + 1) * sub)
            mh, ml = high[k1, mine, :], low[k1, mine, :]
            yh, yl = y_high[k1], y_low[k1]
            value = lax.dot_general(mh, yh, NT, preferred_element_type=jnp.float32)
            value = value + lax.dot_general(mh, yl, NT, preferred_element_type=jnp.float32)
            value = value + lax.dot_general(ml, yh, NT, preferred_element_type=jnp.float32)
            for a in range(inputs):
                spread[pl.ds(p * inputs + a, sub, 2 * inputs), :] = value[:, a * specs : (a + 1) * specs]
        send[k1] = spread[...].astype(jnp.bfloat16).reshape(n, split * rows, specs)
        for h in range(split):
            chunk = k1 * split + h
            cut = pl.ds(h * rows, rows)
            pltpu.make_async_copy(send.at[k1, me, cut], recv.at[chunk, me], recv_sem.at[chunk]).start()

            @pl.loop(0, n - 1)
            def _(i):
                step = (i + 1) // 2
                to = lax.rem(me + n + n // 2 + step * (2 * (i % 2) - 1), n)
                pltpu.make_async_remote_copy(
                    src_ref=send.at[k1, to, cut],
                    dst_ref=recv.at[chunk, me],
                    send_sem=send_sem.at[k1],
                    recv_sem=recv_sem.at[chunk],
                    device_id={"chan": to},
                    device_id_type=pl.DeviceIdType.MESH,
                ).start()

    def exchange(chunk):
        return pltpu.make_async_remote_copy(
            src_ref=part.at[chunk, :, pl.ds(pl.multiple_of((1 - t) * half, half), half), :],
            dst_ref=other.at[chunk],
            send_sem=tm_send_sem.at[chunk],
            recv_sem=tm_recv_sem.at[chunk],
            device_id={"tm": 1 - t},
            device_id_type=pl.DeviceIdType.MESH,
        )

    def finish(chunk):
        exchange(chunk).wait_recv()
        own = part[chunk, :, pl.ds(pl.multiple_of(t * half, half), half), :]
        out_ref[chunk % split, :, chunk // split] = (own + other[chunk]) * (1.0 / (2 * specs))

    @pl.loop(0, chunks)
    def _(chunk):
        pltpu.make_async_copy(recv.at[chunk], recv.at[chunk], recv_sem.at[chunk]).wait()

        @pl.loop(0, pairs)
        def _(j):
            at = pl.multiple_of(j * 4 * inputs, 4 * inputs)
            turned = []
            for g in range(groups):
                block = recv[chunk, g * GROUP : (g + 1) * GROUP, pl.ds(at, 4 * inputs), :]
                block = block.reshape(GROUP * 4 * inputs, specs)
                turned.append(jnp.dot(perm_ref[...], block, preferred_element_type=jnp.float32).astype(jnp.bfloat16))
            run = GROUP * inputs
            for c in range(2):
                real = jnp.concatenate([x[2 * c * run : (2 * c + 1) * run] for x in turned], axis=0)
                imag = jnp.concatenate([x[(2 * c + 1) * run : (2 * c + 2) * run] for x in turned], axis=0)
                left = jnp.concatenate([real, imag], axis=1)
                right = jnp.concatenate([left, jnp.concatenate([-imag, real], axis=1)], axis=0)
                part[chunk, 2 * j + c] = lax.dot_general(left, right, NT, preferred_element_type=jnp.float32)

        exchange(chunk).start()

        @pl.when(chunk > 0)
        def _():
            finish(chunk - 1)

    finish(chunks - 1)

    @pl.when(t == 0)
    def _():
        halo.wait_send()

    @pl.loop(0, chunks)
    def _(chunk):
        exchange(chunk).wait_send()

    @pl.loop(0, RADIX)
    def _(k1):
        pltpu.make_async_copy(send.at[k1, 0 : n - 1], send.at[k1, 0 : n - 1], send_sem.at[k1]).wait()


def local_few(n, voltages):
    inputs = voltages.shape[1]
    specs = voltages.shape[2] // NCH
    tiles = NCH // LANES
    frame = tiles * inputs
    volts = voltages.reshape(2, inputs, specs * tiles, LANES).transpose(0, 2, 1, 3).reshape(2, specs * frame, LANES)
    high, low = make_dft(NCH)
    per = NCH // n // RADIX
    split = SPLIT if per % (2 * SPLIT) == 0 else 1
    chunks, each = RADIX * split, per // split
    total = n * inputs
    rows = each * 2 * inputs
    whole = pl.BlockSpec(memory_space=pltpu.VMEM)
    there = pl.BlockSpec(memory_space=pl.ANY)
    out = pl.pallas_call(
        functools.partial(kernel_few, n, inputs, specs),
        out_shape=jax.ShapeDtypeStruct((split, each, RADIX, total // 2, 2 * total), jnp.float32),
        in_specs=[there, whole, there, there, whole],
        out_specs=whole,
        scratch_shapes=[
            pltpu.VMEM((2, (specs + TAPS - 1) * frame, LANES), jnp.int32),
            pltpu.VMEM((RADIX, NCH // 2, NCH // 2), jnp.bfloat16),
            pltpu.VMEM((RADIX, NCH // 2, NCH // 2), jnp.bfloat16),
            pltpu.VMEM((2, BLOCK * tiles, LANES), jnp.float32),
            pltpu.VMEM((RADIX, inputs * specs, NCH // 2), jnp.bfloat16),
            pltpu.VMEM((RADIX, inputs * specs, NCH // 2), jnp.bfloat16),
            pltpu.VMEM((NCH // RADIX * 2 * inputs, specs), jnp.float32),
            pltpu.VMEM((RADIX, n, split * rows, specs), jnp.bfloat16),
            pltpu.VMEM((chunks, n, rows, specs), jnp.bfloat16),
            pltpu.VMEM((chunks, each, total, 2 * total), jnp.float32),
            pltpu.VMEM((chunks, each, total // 2, 2 * total), jnp.float32),
            pltpu.SemaphoreType.DMA((2,)),
            pltpu.SemaphoreType.DMA((2,)),
            pltpu.SemaphoreType.DMA,
            pltpu.SemaphoreType.DMA,
            pltpu.SemaphoreType.DMA((RADIX,)),
            pltpu.SemaphoreType.DMA((chunks,)),
            pltpu.SemaphoreType.DMA((chunks,)),
            pltpu.SemaphoreType.DMA((chunks,)),
        ],
        compiler_params=pltpu.CompilerParams(
            collective_id=0, has_side_effects=True, vmem_limit_bytes=60 * 1024 * 1024
        ),
    )(
        volts,
        jnp.asarray(make_taps(NCH).reshape(TAPS, tiles, LANES)),
        jnp.asarray(high),
        jnp.asarray(low),
        jnp.asarray(make_permutation(inputs)),
    )
    out = out.reshape(1, RADIX * per, total // 2, 2 * total)
    first = lax.broadcasted_iota(jnp.int32, (2, 1, 1, 1), 0) == 0
    return jnp.where(first, out[..., :total], out[..., total:])


def kernel(
    n,
    inputs,
    specs,
    volts_ref,
    table_ref,
    out_ref,
    raw,
    table,
    taps,
    filtered,
    y_high,
    y_low,
    send,
    recv,
    turned,
    part,
    other,
    result,
    load_sem,
    table_sem,
    halo_send_sem,
    halo_recv_sem,
    send_sem,
    recv_sem,
    tm_send_sem,
    tm_recv_sem,
    out_sem,
):
    me = lax.axis_index("chan")
    t = lax.axis_index("tm")
    sub = NCH // RADIX
    frame = NCH // LANES * inputs
    before = (TAPS - 1) * frame
    split = recv.shape[2]
    chunks = RADIX * split
    total = n * inputs
    half = total // 2

    barrier = pltpu.get_barrier_semaphore()

    @pl.loop(1, n)
    def _(i):
        pl.semaphore_signal(barrier, inc=1, device_id={"chan": lax.rem(me + i, n)}, device_id_type=pl.DeviceIdType.MESH)

    pl.semaphore_signal(barrier, inc=1, device_id={"tm": 1 - t}, device_id_type=pl.DeviceIdType.MESH)

    size = 2 * RADIX * NCH // 2
    early = pltpu.make_async_copy(table_ref.at[size:], table.at[size:], table_sem.at[0])

    def matrices(k1):
        rows = pl.ds(pl.multiple_of(k1 * NCH, NCH), NCH)
        return pltpu.make_async_copy(table_ref.at[rows], table.at[rows], table_sem.at[1 + k1])

    early.start()
    piece = specs * frame // LOADS
    loads = [
        [
            pltpu.make_async_copy(
                volts_ref.at[p, g * piece : (g + 1) * piece, :],
                raw.at[p, before + g * piece : before + (g + 1) * piece, :],
                load_sem.at[g, p],
            )
            for p in range(2)
        ]
        for g in range(LOADS)
    ]
    for group in loads:
        for copy in group:
            copy.start()
    matrices(0).start()

    halo = pltpu.make_async_remote_copy(
        src_ref=volts_ref.at[:, specs * frame - before : specs * frame, :],
        dst_ref=raw.at[:, 0:before, :],
        send_sem=halo_send_sem,
        recv_sem=halo_recv_sem,
        device_id={"tm": 1 - t},
        device_id_type=pl.DeviceIdType.MESH,
    )
    early.wait()
    taps[...] = sum(
        table[size + i * TAPS * 8 : size + (i + 1) * TAPS * 8, 0:LANES].astype(jnp.float32) for i in range(3)
    ).reshape(TAPS, 8, LANES)

    def transform(k1, rows, length, columns):
        at = pl.multiple_of(k1 * NCH + rows, 16)
        mh, ml = table[pl.ds(at, length), :], table[pl.ds(at + NCH // 2, length), :]
        yh, yl = y_high[k1, columns, :], y_low[k1, columns, :]
        value = lax.dot_general(mh, yh, NT, preferred_element_type=jnp.float32)
        value = value + lax.dot_general(mh, yl, NT, preferred_element_type=jnp.float32)
        return value + lax.dot_general(ml, yh, NT, preferred_element_type=jnp.float32)

    mine, place = me // (n // 2), lax.rem(me, n // 2)

    def to_half(k1, cut, sem, far):
        @pl.loop(1 - far, n // 2)
        def _(i):
            side = 1 - mine if far else mine
            to = side * (n // 2) + lax.rem(place + i, n // 2)
            pltpu.make_async_remote_copy(
                src_ref=send.at[(k1, to) + cut],
                dst_ref=recv.at[(k1, me) + cut],
                send_sem=send_sem.at[k1],
                recv_sem=sem,
                device_id={"chan": to},
                device_id_type=pl.DeviceIdType.MESH,
            ).start()

    def to_partners(k1, cut, sem, order):
        for far in order:
            to_half(k1, cut, sem, far)
        pltpu.make_async_copy(send.at[(k1, me) + cut], recv.at[(k1, me) + cut], sem).start()

    many = specs // BLOCK // LOADS

    def filter_some(first, last, a):
        @pl.loop(first, last)
        def _(b):
            filter_block(b, a, inputs, specs, raw, taps, filtered, y_high, y_low)

    for g in range(LOADS):
        for copy in loads[g]:
            copy.wait()
        filter_some(max(1, g * many), (g + 1) * many, 0)
    for k1 in range(1, RADIX):
        matrices(k1).start()

    pl.semaphore_wait(barrier, n)

    @pl.when(t == 0)
    def _():
        halo.start()
        raw[:, 0:before, :] = jnp.zeros((2, before, LANES), jnp.int32)

    filter_some(1, specs // BLOCK, 1)

    @pl.when(t == 1)
    def _():
        halo.wait_recv()

    for pick in [range(a, a + 2) for a in range(0, inputs, 2)]:
        for a in pick:
            filter_some(0, 1 if 0 in pick else specs // BLOCK, a)
        if 0 in pick:
            matrices(0).wait()
        value = transform(0, 0, 2 * sub, slice(pick.start * specs, pick.stop * specs))
        for i, a in enumerate(pick):
            send[0, :, :, a] = value[:, i * specs : (i + 1) * specs].astype(jnp.bfloat16).reshape(n, split, 16, specs)
        to_partners(0, (slice(0, split), slice(pick.start, pick.stop)), recv_sem.at[0], (1, 0))

    def fill(k1):
        matrices(k1).wait()
        for p in range(2):
            value = transform(k1, p * sub, sub, slice(0, inputs * specs))
            for a in range(inputs):
                mine = value[:, a * specs : (a + 1) * specs].astype(jnp.bfloat16)
                send[k1, p * n // 2 : (p + 1) * n // 2, :, a] = mine.reshape(n // 2, split, 16, specs)

    last = RADIX - 1

    @pl.loop(1, last)
    def _(k1):
        fill(k1)
        to_partners(k1, (), recv_sem.at[k1 * split], (1, 0))

    fill(last)
    for h in range(split):
        to_partners(last, (h,), recv_sem.at[last * split + h], (1, 0) if h + 1 < split else (0, 1))

    def exchange(chunk, q):
        return pltpu.make_async_remote_copy(
            src_ref=part.at[chunk, 4 * q : 4 * q + 4, pl.ds(pl.multiple_of((1 - t) * half, half), half), :],
            dst_ref=other.at[chunk, 4 * q : 4 * q + 4],
            send_sem=tm_send_sem.at[chunk, q],
            recv_sem=tm_recv_sem.at[chunk, q],
            device_id={"tm": 1 - t},
            device_id_type=pl.DeviceIdType.MESH,
        )

    def store(chunk, q):
        return pltpu.make_async_copy(
            result.at[chunk, :, 4 * q : 4 * q + 4],
            out_ref.at[:, chunk % split, 4 * q : 4 * q + 4, chunk // split],
            out_sem.at[chunk, q],
        )

    def finish(chunk):
        for q in range(2):
            exchange(chunk, q).wait_recv()
            own = part[chunk, 4 * q : 4 * q + 4, pl.ds(pl.multiple_of(t * half, half), half), :]
            value = (own + other[chunk, 4 * q : 4 * q + 4]) * (1.0 / (2 * specs))
            result[chunk, 0, 4 * q : 4 * q + 4] = value[:, :, :total]
            result[chunk, 1, 4 * q : 4 * q + 4] = value[:, :, total:]
            store(chunk, q).start()

    @pl.loop(0, chunks)
    def _(chunk):
        k1, h = chunk // split, chunk % split

        @pl.when((k1 < last) & (h == 0))
        def _():
            pltpu.make_async_copy(recv.at[k1], recv.at[k1], recv_sem.at[chunk]).wait()

        @pl.when(k1 == last)
        def _():
            came = recv.at[last, :, h]
            pltpu.make_async_copy(came, came, recv_sem.at[chunk]).wait()

        turned[...] = recv[k1, :, h].astype(jnp.float32).reshape(total * 16, specs)
        for c in range(8):
            real = turned[pl.ds(c, total, 16), :].astype(jnp.bfloat16)
            imag = turned[pl.ds(8 + c, total, 16), :].astype(jnp.bfloat16)
            left = jnp.concatenate([real, imag], axis=1)
            right = jnp.concatenate([left, jnp.concatenate([-imag, real], axis=1)], axis=0)
            part[chunk, c] = lax.dot_general(left, right, NT, preferred_element_type=jnp.float32)
            if c % 4 == 3:
                exchange(chunk, c // 4).start()

        @pl.when(chunk > 0)
        def _():
            finish(chunk - 1)

    finish(chunks - 1)

    @pl.when(t == 0)
    def _():
        halo.wait_send()

    @pl.loop(0, chunks)
    def _(chunk):
        for q in range(2):
            exchange(chunk, q).wait_send()
            store(chunk, q).wait()

    @pl.loop(0, RADIX)
    def _(k1):
        pltpu.make_async_copy(send.at[k1, 0 : n - 1], send.at[k1, 0 : n - 1], send_sem.at[k1]).wait()


def local(n, voltages):
    inputs = voltages.shape[1]
    specs = voltages.shape[2] // NCH
    per = NCH // n // RADIX
    if per % 8:
        return local_few(n, voltages)
    tiles = NCH // LANES
    frame = tiles * inputs
    volts = voltages.reshape(2, inputs, specs * tiles, LANES).transpose(0, 2, 1, 3).reshape(2, specs * frame, LANES)
    high, low = make_dft(NCH)
    parts, rest = [], make_taps(NCH).reshape(-1, LANES)
    for _ in range(3):
        parts.append(rest.astype(ml_dtypes.bfloat16))
        rest = rest - parts[-1].astype(np.float32)
    parts = np.pad(np.concatenate(parts), ((0, 0), (0, NCH // 2 - LANES)))
    split = per // 8
    chunks = RADIX * split
    total = n * inputs

    def tiled(m):
        return m.reshape(RADIX, 2, NCH // RADIX // 8, 8, NCH // 2).transpose(0, 2, 1, 3, 4).reshape(m.shape)

    table = np.stack([tiled(high), tiled(low)], axis=1).reshape(-1, NCH // 2)
    table = np.concatenate([table, parts])
    there = pl.BlockSpec(memory_space=pltpu.HBM)
    out = pl.pallas_call(
        functools.partial(kernel, n, inputs, specs),
        out_shape=jax.ShapeDtypeStruct((2, split, 8, RADIX, total // 2, total), jnp.float32),
        in_specs=[there, there],
        out_specs=pl.BlockSpec(memory_space=pl.ANY),
        scratch_shapes=[
            pltpu.VMEM((2, (specs + TAPS - 1) * frame, LANES), jnp.int32),
            pltpu.VMEM(table.shape, jnp.bfloat16),
            pltpu.VMEM((TAPS, tiles, LANES), jnp.float32),
            pltpu.VMEM((2, BLOCK * tiles, LANES), jnp.float32),
            pltpu.VMEM((RADIX, inputs * specs, NCH // 2), jnp.bfloat16),
            pltpu.VMEM((RADIX, inputs * specs, NCH // 2), jnp.bfloat16),
            pltpu.VMEM((RADIX, n, split, inputs, 16, specs), jnp.bfloat16),
            pltpu.VMEM((RADIX, n, split, inputs, 16, specs), jnp.bfloat16),
            pltpu.VMEM((total * 16, specs), jnp.float32),
            pltpu.VMEM((chunks, 8, total, 2 * total), jnp.float32),
            pltpu.VMEM((chunks, 8, total // 2, 2 * total), jnp.float32),
            pltpu.VMEM((chunks, 2, 8, total // 2, total), jnp.float32),
            pltpu.SemaphoreType.DMA((LOADS, 2)),
            pltpu.SemaphoreType.DMA((1 + RADIX,)),
            pltpu.SemaphoreType.DMA,
            pltpu.SemaphoreType.DMA,
            pltpu.SemaphoreType.DMA((RADIX,)),
            pltpu.SemaphoreType.DMA((chunks,)),
            pltpu.SemaphoreType.DMA((chunks, 2)),
            pltpu.SemaphoreType.DMA((chunks, 2)),
            pltpu.SemaphoreType.DMA((chunks, 2)),
        ],
        compiler_params=pltpu.CompilerParams(
            collective_id=0, has_side_effects=True, vmem_limit_bytes=VMEM * 1024 * 1024
        ),
    )(volts, jnp.asarray(table))
    return out.reshape(2, RADIX * per, total // 2, total)


def solution(mesh):
    placed = (P(None, "chan", "tm"),)
    return jax.shard_map(
        functools.partial(local, mesh.shape["chan"]),
        mesh=mesh,
        in_specs=placed,
        out_specs=P(None, "chan", "tm", None),
        check_vma=False,
    )
```

```python
import functools

import jax
import jax.numpy as jnp
import ml_dtypes
import numpy as np
from jax import lax
from jax.experimental import pallas as pl
from jax.experimental.pallas import tpu as pltpu
from jax.sharding import PartitionSpec as P

NCH = 1024
TAPS = 4
RADIX = 4
GROUP = 16
LANES = 128
BLOCK = 16
SPLIT = 2
LOADS = 4
VMEM = 50
NT = (((1,), (1,)), ((), ()))


def make_taps(nch):
    k = np.arange(TAPS * nch, dtype=np.float64)
    x = (k - 2.0 * nch + 0.5) / nch
    window = 0.54 - 0.46 * np.cos(2.0 * np.pi * (k + 0.5) / (TAPS * nch))
    return (np.sinc(x) * window).reshape(TAPS, nch).astype(np.float32)


def make_dft(nch):
    sub = nch // RADIX
    n = np.arange(sub)
    highs, lows = [], []
    for r in range(RADIX):
        k = RADIX * np.arange(sub) + r
        angle = (k[:, None] * n[None, :] % nch) * (2.0 * np.pi / nch)
        c, s = np.cos(angle), np.sin(angle)
        m = np.block([[c, s], [-s, c]]) * (0.25 / np.sqrt(nch))
        high = m.astype(np.float32).astype(ml_dtypes.bfloat16)
        low = (m - high.astype(np.float64)).astype(np.float32).astype(ml_dtypes.bfloat16)
        highs.append(high)
        lows.append(low)
    return np.stack(highs), np.stack(lows)


def make_permutation(local_inputs):
    size = GROUP * 4 * local_inputs
    order = np.arange(size).reshape(GROUP, 2, 2, local_inputs).transpose(1, 2, 0, 3).reshape(-1)
    perm = np.zeros((size, size), np.float32)
    perm[np.arange(size), order] = 1.0
    return perm.astype(ml_dtypes.bfloat16)


def filter_block(b, a, inputs, specs, raw, taps_ref, filtered, y_high, y_low):
    sub = NCH // RADIX
    tiles = NCH // LANES
    frame = tiles * inputs
    at = b * BLOCK
    for p in range(2):
        frames = raw[p, pl.ds(at * frame + a, (BLOCK + TAPS - 1) * tiles, inputs), :].astype(jnp.float32)
        frames = frames.reshape(BLOCK + TAPS - 1, tiles, LANES)
        value = taps_ref[0] * frames[0:BLOCK]
        for step in range(1, TAPS):
            value = value + taps_ref[step] * frames[step : step + BLOCK]
        filtered[p] = value.reshape(BLOCK * tiles, LANES)
    quarter = tiles // RADIX
    place = pl.ds(pl.multiple_of(a * specs + at, BLOCK), BLOCK)
    for h in range(quarter):
        r, im = [[filtered[p, pl.ds(q * quarter + h, BLOCK, tiles), :] for q in range(RADIX)] for p in range(2)]
        er, orr, dr, gr = r[0] + r[2], r[1] + r[3], r[0] - r[2], r[1] - r[3]
        ei, oi, di, gi = im[0] + im[2], im[1] + im[3], im[0] - im[2], im[1] - im[3]
        parts = [(er + orr, ei + oi), (dr + gi, di - gr), (er - orr, ei - oi), (dr - gi, di + gr)]
        for k1 in range(RADIX):
            for p in range(2):
                value = parts[k1][p]
                top = value.astype(jnp.bfloat16)
                lanes = slice(p * sub + h * LANES, p * sub + (h + 1) * LANES)
                y_high[k1, place, lanes] = top
                y_low[k1, place, lanes] = (value - top.astype(jnp.float32)).astype(jnp.bfloat16)


def kernel_few(
    n,
    inputs,
    specs,
    volts_ref,
    taps_ref,
    high_ref,
    low_ref,
    perm_ref,
    out_ref,
    raw,
    high,
    low,
    filtered,
    y_high,
    y_low,
    spread,
    send,
    recv,
    part,
    other,
    load_sem,
    table_sem,
    halo_send_sem,
    halo_recv_sem,
    send_sem,
    recv_sem,
    tm_send_sem,
    tm_recv_sem,
):
    me = lax.axis_index("chan")
    t = lax.axis_index("tm")
    sub = NCH // RADIX
    tiles = NCH // LANES
    frame = tiles * inputs
    before = (TAPS - 1) * frame
    chunks = recv.shape[0]
    split = chunks // RADIX
    rows = recv.shape[2]
    pairs = rows // (4 * inputs)
    groups = n // GROUP
    half = n * inputs // 2

    barrier = pltpu.get_barrier_semaphore()

    @pl.loop(1, n)
    def _(i):
        pl.semaphore_signal(barrier, inc=1, device_id={"chan": lax.rem(me + i, n)}, device_id_type=pl.DeviceIdType.MESH)

    pl.semaphore_signal(barrier, inc=1, device_id={"tm": 1 - t}, device_id_type=pl.DeviceIdType.MESH)

    loads = [
        pltpu.make_async_copy(volts_ref.at[p], raw.at[p, before : before + specs * frame, :], load_sem.at[p])
        for p in range(2)
    ]
    tables = [
        pltpu.make_async_copy(high_ref, high, table_sem.at[0]),
        pltpu.make_async_copy(low_ref, low, table_sem.at[1]),
    ]
    for copy in loads + tables:
        copy.start()

    halo = pltpu.make_async_remote_copy(
        src_ref=volts_ref.at[:, specs * frame - before : specs * frame, :],
        dst_ref=raw.at[:, 0:before, :],
        send_sem=halo_send_sem,
        recv_sem=halo_recv_sem,
        device_id={"tm": 1 - t},
        device_id_type=pl.DeviceIdType.MESH,
    )
    pl.semaphore_wait(barrier, n)

    @pl.when(t == 0)
    def _():
        halo.start()
        raw[:, 0:before, :] = jnp.zeros((2, before, LANES), jnp.int32)

    for copy in loads:
        copy.wait()

    @pl.loop(1, specs // BLOCK)
    def _(b):
        for a in range(inputs):
            filter_block(b, a, inputs, specs, raw, taps_ref, filtered, y_high, y_low)

    @pl.when(t == 1)
    def _():
        halo.wait_recv()

    for a in range(inputs):
        filter_block(0, a, inputs, specs, raw, taps_ref, filtered, y_high, y_low)

    for copy in tables:
        copy.wait()

    @pl.loop(0, RADIX)
    def _(k1):
        for p in range(2):
            mine = slice(p * sub, (p + 1) * sub)
            mh, ml = high[k1, mine, :], low[k1, mine, :]
            yh, yl = y_high[k1], y_low[k1]
            value = lax.dot_general(mh, yh, NT, preferred_element_type=jnp.float32)
            value = value + lax.dot_general(mh, yl, NT, preferred_element_type=jnp.float32)
            value = value + lax.dot_general(ml, yh, NT, preferred_element_type=jnp.float32)
            for a in range(inputs):
                spread[pl.ds(p * inputs + a, sub, 2 * inputs), :] = value[:, a * specs : (a + 1) * specs]
        send[k1] = spread[...].astype(jnp.bfloat16).reshape(n, split * rows, specs)
        for h in range(split):
            chunk = k1 * split + h
            cut = pl.ds(h * rows, rows)
            pltpu.make_async_copy(send.at[k1, me, cut], recv.at[chunk, me], recv_sem.at[chunk]).start()

            @pl.loop(0, n - 1)
            def _(i):
                step = (i + 1) // 2
                to = lax.rem(me + n + n // 2 + step * (2 * (i % 2) - 1), n)
                pltpu.make_async_remote_copy(
                    src_ref=send.at[k1, to, cut],
                    dst_ref=recv.at[chunk, me],
                    send_sem=send_sem.at[k1],
                    recv_sem=recv_sem.at[chunk],
                    device_id={"chan": to},
                    device_id_type=pl.DeviceIdType.MESH,
                ).start()

    def exchange(chunk):
        return pltpu.make_async_remote_copy(
            src_ref=part.at[chunk, :, pl.ds(pl.multiple_of((1 - t) * half, half), half), :],
            dst_ref=other.at[chunk],
            send_sem=tm_send_sem.at[chunk],
            recv_sem=tm_recv_sem.at[chunk],
            device_id={"tm": 1 - t},
            device_id_type=pl.DeviceIdType.MESH,
        )

    def finish(chunk):
        exchange(chunk).wait_recv()
        own = part[chunk, :, pl.ds(pl.multiple_of(t * half, half), half), :]
        out_ref[chunk % split, :, chunk // split] = (own + other[chunk]) * (1.0 / (2 * specs))

    @pl.loop(0, chunks)
    def _(chunk):
        pltpu.make_async_copy(recv.at[chunk], recv.at[chunk], recv_sem.at[chunk]).wait()

        @pl.loop(0, pairs)
        def _(j):
            at = pl.multiple_of(j * 4 * inputs, 4 * inputs)
            turned = []
            for g in range(groups):
                block = recv[chunk, g * GROUP : (g + 1) * GROUP, pl.ds(at, 4 * inputs), :]
                block = block.reshape(GROUP * 4 * inputs, specs)
                turned.append(jnp.dot(perm_ref[...], block, preferred_element_type=jnp.float32).astype(jnp.bfloat16))
            run = GROUP * inputs
            for c in range(2):
                real = jnp.concatenate([x[2 * c * run : (2 * c + 1) * run] for x in turned], axis=0)
                imag = jnp.concatenate([x[(2 * c + 1) * run : (2 * c + 2) * run] for x in turned], axis=0)
                left = jnp.concatenate([real, imag], axis=1)
                right = jnp.concatenate([left, jnp.concatenate([-imag, real], axis=1)], axis=0)
                part[chunk, 2 * j + c] = lax.dot_general(left, right, NT, preferred_element_type=jnp.float32)

        exchange(chunk).start()

        @pl.when(chunk > 0)
        def _():
            finish(chunk - 1)

    finish(chunks - 1)

    @pl.when(t == 0)
    def _():
        halo.wait_send()

    @pl.loop(0, chunks)
    def _(chunk):
        exchange(chunk).wait_send()

    @pl.loop(0, RADIX)
    def _(k1):
        pltpu.make_async_copy(send.at[k1, 0 : n - 1], send.at[k1, 0 : n - 1], send_sem.at[k1]).wait()


def local_few(n, voltages):
    inputs = voltages.shape[1]
    specs = voltages.shape[2] // NCH
    tiles = NCH // LANES
    frame = tiles * inputs
    volts = voltages.reshape(2, inputs, specs * tiles, LANES).transpose(0, 2, 1, 3).reshape(2, specs * frame, LANES)
    high, low = make_dft(NCH)
    per = NCH // n // RADIX
    split = SPLIT if per % (2 * SPLIT) == 0 else 1
    chunks, each = RADIX * split, per // split
    total = n * inputs
    rows = each * 2 * inputs
    whole = pl.BlockSpec(memory_space=pltpu.VMEM)
    there = pl.BlockSpec(memory_space=pl.ANY)
    out = pl.pallas_call(
        functools.partial(kernel_few, n, inputs, specs),
        out_shape=jax.ShapeDtypeStruct((split, each, RADIX, total // 2, 2 * total), jnp.float32),
        in_specs=[there, whole, there, there, whole],
        out_specs=whole,
        scratch_shapes=[
            pltpu.VMEM((2, (specs + TAPS - 1) * frame, LANES), jnp.int32),
            pltpu.VMEM((RADIX, NCH // 2, NCH // 2), jnp.bfloat16),
            pltpu.VMEM((RADIX, NCH // 2, NCH // 2), jnp.bfloat16),
            pltpu.VMEM((2, BLOCK * tiles, LANES), jnp.float32),
            pltpu.VMEM((RADIX, inputs * specs, NCH // 2), jnp.bfloat16),
            pltpu.VMEM((RADIX, inputs * specs, NCH // 2), jnp.bfloat16),
            pltpu.VMEM((NCH // RADIX * 2 * inputs, specs), jnp.float32),
            pltpu.VMEM((RADIX, n, split * rows, specs), jnp.bfloat16),
            pltpu.VMEM((chunks, n, rows, specs), jnp.bfloat16),
            pltpu.VMEM((chunks, each, total, 2 * total), jnp.float32),
            pltpu.VMEM((chunks, each, total // 2, 2 * total), jnp.float32),
            pltpu.SemaphoreType.DMA((2,)),
            pltpu.SemaphoreType.DMA((2,)),
            pltpu.SemaphoreType.DMA,
            pltpu.SemaphoreType.DMA,
            pltpu.SemaphoreType.DMA((RADIX,)),
            pltpu.SemaphoreType.DMA((chunks,)),
            pltpu.SemaphoreType.DMA((chunks,)),
            pltpu.SemaphoreType.DMA((chunks,)),
        ],
        compiler_params=pltpu.CompilerParams(
            collective_id=0, has_side_effects=True, vmem_limit_bytes=60 * 1024 * 1024
        ),
    )(
        volts,
        jnp.asarray(make_taps(NCH).reshape(TAPS, tiles, LANES)),
        jnp.asarray(high),
        jnp.asarray(low),
        jnp.asarray(make_permutation(inputs)),
    )
    out = out.reshape(1, RADIX * per, total // 2, 2 * total)
    first = lax.broadcasted_iota(jnp.int32, (2, 1, 1, 1), 0) == 0
    return jnp.where(first, out[..., :total], out[..., total:])


def kernel(
    n,
    inputs,
    specs,
    volts_ref,
    table_ref,
    out_ref,
    raw,
    table,
    taps,
    filtered,
    y_high,
    y_low,
    send,
    recv,
    turned,
    part,
    other,
    result,
    load_sem,
    table_sem,
    halo_send_sem,
    halo_recv_sem,
    send_sem,
    recv_sem,
    tm_send_sem,
    tm_recv_sem,
    out_sem,
):
    me = lax.axis_index("chan")
    t = lax.axis_index("tm")
    sub = NCH // RADIX
    frame = NCH // LANES * inputs
    before = (TAPS - 1) * frame
    split = recv.shape[3]
    chunks = RADIX * split
    total = n * inputs
    half = total // 2

    barrier = pltpu.get_barrier_semaphore()

    @pl.loop(1, n)
    def _(i):
        pl.semaphore_signal(barrier, inc=1, device_id={"chan": lax.rem(me + i, n)}, device_id_type=pl.DeviceIdType.MESH)

    pl.semaphore_signal(barrier, inc=1, device_id={"tm": 1 - t}, device_id_type=pl.DeviceIdType.MESH)

    size = 2 * RADIX * NCH // 2
    early = pltpu.make_async_copy(table_ref.at[size:], table.at[size:], table_sem.at[0])

    def matrices(k1):
        rows = pl.ds(pl.multiple_of(k1 * NCH, NCH), NCH)
        return pltpu.make_async_copy(table_ref.at[rows], table.at[rows], table_sem.at[1 + k1])

    early.start()
    piece = specs * frame // LOADS
    loads = [
        [
            pltpu.make_async_copy(
                volts_ref.at[p, g * piece : (g + 1) * piece, :],
                raw.at[p, before + g * piece : before + (g + 1) * piece, :],
                load_sem.at[g, p],
            )
            for p in range(2)
        ]
        for g in range(LOADS)
    ]
    for group in loads:
        for copy in group:
            copy.start()
    matrices(0).start()

    halo = pltpu.make_async_remote_copy(
        src_ref=volts_ref.at[:, specs * frame - before : specs * frame, :],
        dst_ref=raw.at[:, 0:before, :],
        send_sem=halo_send_sem,
        recv_sem=halo_recv_sem,
        device_id={"tm": 1 - t},
        device_id_type=pl.DeviceIdType.MESH,
    )
    pl.semaphore_wait(barrier, n)

    @pl.when(t == 0)
    def _():
        halo.start()
        raw[:, 0:before, :] = jnp.zeros((2, before, LANES), jnp.int32)

    early.wait()
    taps[...] = sum(
        table[size + i * TAPS * 8 : size + (i + 1) * TAPS * 8, 0:LANES].astype(jnp.float32) for i in range(3)
    ).reshape(TAPS, 8, LANES)

    def transform(k1, rows, length, columns):
        at = pl.multiple_of(k1 * NCH + rows, 16)
        mh, ml = table[pl.ds(at, length), :], table[pl.ds(at + NCH // 2, length), :]
        yh, yl = y_high[k1, columns, :], y_low[k1, columns, :]
        value = lax.dot_general(mh, yh, NT, preferred_element_type=jnp.float32)
        value = value + lax.dot_general(mh, yl, NT, preferred_element_type=jnp.float32)
        return value + lax.dot_general(ml, yh, NT, preferred_element_type=jnp.float32)

    mine, place = me // (n // 2), lax.rem(me, n // 2)

    def to_partners(k1, cut, sem):
        def give(to):
            pltpu.make_async_remote_copy(
                src_ref=send.at[(k1, to) + cut],
                dst_ref=recv.at[(k1, me) + cut],
                send_sem=send_sem.at[k1],
                recv_sem=sem,
                device_id={"chan": to},
                device_id_type=pl.DeviceIdType.MESH,
            ).start()

        give((1 - mine) * (n // 2) + place)

        @pl.loop(1, n // 2)
        def _(i):
            step = lax.rem(place + i, n // 2)
            give(mine * (n // 2) + step)
            give((1 - mine) * (n // 2) + step)

        pltpu.make_async_copy(send.at[(k1, me) + cut], recv.at[(k1, me) + cut], sem).start()

    for pick in [range(0, 1), range(1, 2)] + [range(a, a + 2) for a in range(2, inputs, 2)]:

        many = specs // BLOCK // LOADS
        for g in range(LOADS):
            if 0 in pick:
                for copy in loads[g]:
                    copy.wait()
                if g == LOADS - 1:
                    for k1 in range(1, RADIX):
                        matrices(k1).start()

            @pl.loop(max(1, g * many), (g + 1) * many)
            def _(b):
                for a in pick:
                    filter_block(b, a, inputs, specs, raw, taps, filtered, y_high, y_low)

        if 0 in pick:

            @pl.when(t == 1)
            def _():
                halo.wait_recv()

        for a in pick:
            filter_block(0, a, inputs, specs, raw, taps, filtered, y_high, y_low)
        if 0 in pick:
            matrices(0).wait()
        value = transform(0, 0, 2 * sub, slice(pick.start * specs, pick.stop * specs))
        for i, a in enumerate(pick):
            send[0, :, a] = value[:, i * specs : (i + 1) * specs].astype(jnp.bfloat16).reshape(n, split, 16, specs)
        to_partners(0, (slice(pick.start, pick.stop),), recv_sem.at[0])

    @pl.loop(1, RADIX)
    def _(k1):
        matrices(k1).wait()
        for p in range(2):
            value = transform(k1, p * sub, sub, slice(0, inputs * specs))
            for a in range(inputs):
                mine = value[:, a * specs : (a + 1) * specs].astype(jnp.bfloat16)
                send[k1, p * n // 2 : (p + 1) * n // 2, a] = mine.reshape(n // 2, split, 16, specs)
        for h in range(split):
            to_partners(k1, (slice(0, inputs), h), recv_sem.at[k1 * split + h])

    def exchange(chunk, q):
        return pltpu.make_async_remote_copy(
            src_ref=part.at[chunk, 4 * q : 4 * q + 4, pl.ds(pl.multiple_of((1 - t) * half, half), half), :],
            dst_ref=other.at[chunk, 4 * q : 4 * q + 4],
            send_sem=tm_send_sem.at[chunk, q],
            recv_sem=tm_recv_sem.at[chunk, q],
            device_id={"tm": 1 - t},
            device_id_type=pl.DeviceIdType.MESH,
        )

    def store(chunk, q):
        return pltpu.make_async_copy(
            result.at[chunk, :, 4 * q : 4 * q + 4],
            out_ref.at[:, chunk % split, 4 * q : 4 * q + 4, chunk // split],
            out_sem.at[chunk, q],
        )

    def finish(chunk):
        for q in range(2):
            exchange(chunk, q).wait_recv()
            own = part[chunk, 4 * q : 4 * q + 4, pl.ds(pl.multiple_of(t * half, half), half), :]
            value = (own + other[chunk, 4 * q : 4 * q + 4]) * (1.0 / (2 * specs))
            result[chunk, 0, 4 * q : 4 * q + 4] = value[:, :, :total]
            result[chunk, 1, 4 * q : 4 * q + 4] = value[:, :, total:]
            store(chunk, q).start()

    @pl.loop(0, chunks)
    def _(chunk):
        k1, h = chunk // split, chunk % split

        @pl.when(chunk == 0)
        def _():
            pltpu.make_async_copy(recv.at[0], recv.at[0], recv_sem.at[0]).wait()

        @pl.when(chunk >= split)
        def _():
            came = recv.at[k1, :, :, h]
            pltpu.make_async_copy(came, came, recv_sem.at[chunk]).wait()

        turned[...] = recv[k1, :, :, h].astype(jnp.float32).reshape(total * 16, specs)
        for c in range(8):
            real = turned[pl.ds(c, total, 16), :].astype(jnp.bfloat16)
            imag = turned[pl.ds(8 + c, total, 16), :].astype(jnp.bfloat16)
            left = jnp.concatenate([real, imag], axis=1)
            right = jnp.concatenate([left, jnp.concatenate([-imag, real], axis=1)], axis=0)
            part[chunk, c] = lax.dot_general(left, right, NT, preferred_element_type=jnp.float32)
            if c % 4 == 3:
                exchange(chunk, c // 4).start()

        @pl.when(chunk > 0)
        def _():
            finish(chunk - 1)

    finish(chunks - 1)

    @pl.when(t == 0)
    def _():
        halo.wait_send()

    @pl.loop(0, chunks)
    def _(chunk):
        for q in range(2):
            exchange(chunk, q).wait_send()
            store(chunk, q).wait()

    @pl.loop(0, RADIX)
    def _(k1):
        pltpu.make_async_copy(send.at[k1, 0 : n - 1], send.at[k1, 0 : n - 1], send_sem.at[k1]).wait()


def local(n, voltages):
    inputs = voltages.shape[1]
    specs = voltages.shape[2] // NCH
    per = NCH // n // RADIX
    if per % 8:
        return local_few(n, voltages)
    tiles = NCH // LANES
    frame = tiles * inputs
    volts = voltages.reshape(2, inputs, specs * tiles, LANES).transpose(0, 2, 1, 3).reshape(2, specs * frame, LANES)
    high, low = make_dft(NCH)
    parts, rest = [], make_taps(NCH).reshape(-1, LANES)
    for _ in range(3):
        parts.append(rest.astype(ml_dtypes.bfloat16))
        rest = rest - parts[-1].astype(np.float32)
    parts = np.pad(np.concatenate(parts), ((0, 0), (0, NCH // 2 - LANES)))
    split = per // 8
    chunks = RADIX * split
    total = n * inputs

    def tiled(m):
        return m.reshape(RADIX, 2, NCH // RADIX // 8, 8, NCH // 2).transpose(0, 2, 1, 3, 4).reshape(m.shape)

    table = np.stack([tiled(high), tiled(low)], axis=1).reshape(-1, NCH // 2)
    table = np.concatenate([table, parts])
    there = pl.BlockSpec(memory_space=pltpu.HBM)
    out = pl.pallas_call(
        functools.partial(kernel, n, inputs, specs),
        out_shape=jax.ShapeDtypeStruct((2, split, 8, RADIX, total // 2, total), jnp.float32),
        in_specs=[there, there],
        out_specs=pl.BlockSpec(memory_space=pl.ANY),
        scratch_shapes=[
            pltpu.VMEM((2, (specs + TAPS - 1) * frame, LANES), jnp.int32),
            pltpu.VMEM(table.shape, jnp.bfloat16),
            pltpu.VMEM((TAPS, tiles, LANES), jnp.float32),
            pltpu.VMEM((2, BLOCK * tiles, LANES), jnp.float32),
            pltpu.VMEM((RADIX, inputs * specs, NCH // 2), jnp.bfloat16),
            pltpu.VMEM((RADIX, inputs * specs, NCH // 2), jnp.bfloat16),
            pltpu.VMEM((RADIX, n, inputs, split, 16, specs), jnp.bfloat16),
            pltpu.VMEM((RADIX, n, inputs, split, 16, specs), jnp.bfloat16),
            pltpu.VMEM((total * 16, specs), jnp.float32),
            pltpu.VMEM((chunks, 8, total, 2 * total), jnp.float32),
            pltpu.VMEM((chunks, 8, total // 2, 2 * total), jnp.float32),
            pltpu.VMEM((chunks, 2, 8, total // 2, total), jnp.float32),
            pltpu.SemaphoreType.DMA((LOADS, 2)),
            pltpu.SemaphoreType.DMA((1 + RADIX,)),
            pltpu.SemaphoreType.DMA,
            pltpu.SemaphoreType.DMA,
            pltpu.SemaphoreType.DMA((RADIX,)),
            pltpu.SemaphoreType.DMA((chunks,)),
            pltpu.SemaphoreType.DMA((chunks, 2)),
            pltpu.SemaphoreType.DMA((chunks, 2)),
            pltpu.SemaphoreType.DMA((chunks, 2)),
        ],
        compiler_params=pltpu.CompilerParams(
            collective_id=0, has_side_effects=True, vmem_limit_bytes=VMEM * 1024 * 1024
        ),
    )(volts, jnp.asarray(table))
    return out.reshape(2, RADIX * per, total // 2, total)


def solution(mesh):
    placed = (P(None, "chan", "tm"),)
    return jax.shard_map(
        functools.partial(local, mesh.shape["chan"]),
        mesh=mesh,
        in_specs=placed,
        out_specs=P(None, "chan", "tm", None),
        check_vma=False,
    )
```
